128 devices in a mesh: grp: 4 (over z), tp: 32 (over y, x, core).
Axes of the slice: x: 4, y: 4, z: 4, core: 2. Of those that a mesh axis runs over, the one named last changes fastest.
Arguments:
- residual: bfloat16 [1024, 7168], P(('grp', 'tp')), may hold values from -64 to 64
- queries: bfloat16 [1024, 73728], P(('grp', 'tp')), may hold values from -64 to 64
- fresh_latents: bfloat16 [1024, 576], P(('grp', 'tp')), may hold values from -8 to 8
- cache_pages: bfloat16 [8192, 36864], P(('grp', 'tp')), may hold values from -6 to 6
- prefill_pages: bfloat16 [2048, 36864], P(('grp', 'tp')), may hold values from -6 to 6
- prefill_owner: int32 [2048], P(('grp', 'tp')), may hold values from 0 to 3, as said below
- prefill_slot: int32 [2048], P(('grp', 'tp')), may hold values from 0 to 15, as said below
- page_lists: int32 [512, 40], P(('grp', 'tp')), may hold values from 0 to 79, as said below
- context_len: int32 [512], P(('grp', 'tp')), may hold values from 1 to 2560, as said below
- value_up: bfloat16 [128, 512, 128], P('tp'), may hold values from -0.25 to 0.25
- out_proj: bfloat16 [16384, 7168], P('tp'), may hold values from -0.1875 to 0.1875
- norm_gain: bfloat16 [7168], replicated, may hold values from 0.5 to 1.5
- gate_weight: bfloat16 [7168, 9216], P(None, 'tp'), may hold values from -0.0625 to 0.0625
- up_weight: bfloat16 [7168, 9216], P(None, 'tp'), may hold values from -0.0625 to 0.0625
- down_weight: bfloat16 [9216, 7168], P('tp'), may hold values from -0.0625 to 0.0625
Outputs:
- layer_out: bfloat16 [1024, 7168], P(('grp', 'tp'))
The draws below stay inside these ranges and needn't reach their ends.
Inputs may be any that keep to these rules, and one draw needn't show every extreme that they name: `prefill_owner`: within one tp index, every device receives exactly 16 prefilled pages in all, and one device sends at most 8 pages to one owner. `prefill_slot`: the received places of one owner's pages are all different. `page_lists`: entries below 64 name resident pages, 64 + s the received page s. The first ceil(context_len / 64) entries of a row are used, distinct over one device's requests; every received page is used; other entries are 0. `context_len`: every request has at least one cached position.
All inputs are finite; a program needn't handle non-finite values.
Results may differ from the reference program's by a relative error of at most 0.019.
Values may be sent and summed in bfloat16 or wider, within the bound.
No kernel may reach another device: no remote copies, remote signals or barrier semaphores. Data moves between devices by JAX's collectives and lax.ppermute only.
A program may use at most 128 MiB of HBM per device.

```python
import jax
import jax.numpy as jnp
from jax import lax

D = 7168
FF = 9216
HEADS = 128
LAT = 512
ROPE = 64
HEADV = 128
PAGE = 64
REQ_DEV = 4
RES_DEV = 64
PRE_DEV = 16
KVW = 576
MOST = 8
POOL = 80
MAXP = 40
REQUESTS = 512
TOKENS = 1024
N_GRP = 4
N_TP = 32


def page_plan(key):
    devices = N_GRP * N_TP
    chosen_dev = jax.random.randint(jax.random.fold_in(key, 101), (), 0, devices)
    dev_keys = jax.random.split(jax.random.fold_in(key, 102), devices)

    def per_device(dev_key, dev_index):
        subkeys = jax.random.split(dev_key, 7)
        heavy = (jax.random.randint(subkeys[0], (), 0, 4) == 0) | (dev_index == chosen_dev)
        heavy_slot = jax.random.randint(subkeys[1], (), 0, REQ_DEV)
        light_counts = jax.random.randint(subkeys[2], (REQ_DEV,), (PRE_DEV + REQ_DEV - 1) // REQ_DEV, POOL // REQ_DEV + 1)
        others = jax.random.randint(subkeys[3], (REQ_DEV,), 1, (POOL - MAXP) // (REQ_DEV - 1) + 1)
        slot_ids = jnp.arange(REQ_DEV, dtype=jnp.int32)
        heavy_counts = jnp.where(slot_ids == heavy_slot, MAXP, others)
        counts = jnp.where(heavy, heavy_counts, light_counts).astype(jnp.int32)
        used_total = jnp.sum(counts)
        order_first = jax.random.permutation(subkeys[4], POOL)
        pool_ids = jnp.arange(POOL, dtype=jnp.int32)
        ranked = jnp.argsort(jnp.where(pool_ids >= RES_DEV, order_first, POOL + order_first))
        order_second = jax.random.permutation(subkeys[5], POOL)
        shuffled = jnp.argsort(jnp.where(pool_ids < used_total, order_second, POOL + pool_ids))
        chosen_pages = ranked[shuffled].astype(jnp.int32)
        starts = jnp.cumsum(counts) - counts
        where_at = starts[:, None] + jnp.arange(MAXP, dtype=jnp.int32)[None, :]
        in_use = jnp.arange(MAXP, dtype=jnp.int32)[None, :] < counts[:, None]
        page_rows = jnp.where(in_use, chosen_pages[jnp.minimum(where_at, POOL - 1)], 0)
        trimmed = jax.random.randint(subkeys[6], (REQ_DEV,), 0, PAGE)
        trimmed = jnp.where(heavy & (slot_ids == heavy_slot), 0, trimmed)
        return (page_rows.astype(jnp.int32), (counts * PAGE - trimmed).astype(jnp.int32))
    page_rows, lengths = jax.vmap(per_device)(dev_keys, jnp.arange(devices, dtype=jnp.int32))
    return (page_rows.reshape(devices * REQ_DEV, MAXP), lengths.reshape(devices * REQ_DEV))


def owner_plan(key):
    col_keys = jax.random.split(jax.random.fold_in(key, 201), N_TP)

    def column(col_key):
        subkeys = jax.random.split(col_key, 5)
        remain = PRE_DEV - MOST
        cut_points = jnp.sort(jax.random.randint(subkeys[0], (N_GRP - 2,), 0, remain + 1))
        pieces = jnp.diff(jnp.concatenate([jnp.zeros((1,), jnp.int32), cut_points.astype(jnp.int32), jnp.full((1,), remain, jnp.int32)]))
        weights = jax.random.permutation(subkeys[1], jnp.concatenate([jnp.full((1,), MOST, jnp.int32), pieces]))
        rotation = jax.random.randint(subkeys[2], (), 0, N_GRP)
        labels = jnp.arange(N_GRP, dtype=jnp.int32)
        counts = weights[(labels[None, :] - labels[:, None] + rotation) % N_GRP]
        bounds = jnp.cumsum(counts, 1)
        position = jnp.arange(PRE_DEV, dtype=jnp.int32)
        sorted_owners = jnp.sum((bounds[:, None, :] <= position[None, :, None]).astype(jnp.int32), 2)
        shuffles = jax.vmap(lambda mix_key: jax.random.permutation(mix_key, PRE_DEV))(jax.random.split(subkeys[3], N_GRP))
        owners = jnp.take_along_axis(sorted_owners, shuffles, 1)
        matches = (owners[:, :, None] == labels[None, None, :]).astype(jnp.int32)
        order_in = jnp.sum((jnp.cumsum(matches, 1) - matches) * matches, 2)
        offsets = jnp.cumsum(counts, 0) - counts
        raw_slot = jnp.take_along_axis(offsets, owners, 1) + order_in
        spread_slots = jax.vmap(lambda mix_key: jax.random.permutation(mix_key, PRE_DEV))(jax.random.split(subkeys[4], N_GRP))
        slots = spread_slots[owners, raw_slot]
        return (owners.astype(jnp.int32), slots.astype(jnp.int32))
    owners, slots = jax.vmap(column)(col_keys)
    return (jnp.transpose(owners, (1, 0, 2)).reshape(-1), jnp.transpose(slots, (1, 0, 2)).reshape(-1))


def fresh_plan(key, pull_weight):
    subkeys = jax.random.split(jax.random.fold_in(key, 301), 3)
    start_rows = jnp.clip(jax.random.normal(subkeys[0], (REQUESTS, 2, KVW)), -6.0, 6.0)
    chosen = (jax.random.randint(subkeys[1], (REQUESTS,), 0, 3) == 0).astype(jnp.float32)
    head_pick = (jax.random.randint(subkeys[2], (HEADS,), 0, 4) == 0).astype(jnp.float32)
    second_row = start_rows[:, 1]
    fresh_keys = jnp.stack([start_rows[:, 0], second_row], 1)
    aligned = pull_weight * chosen[:, None] * head_pick[None, :]
    return (fresh_keys, aligned)


def draw_residual(key, part):
    key = jax.random.fold_in(key, 5)
    subkeys = jax.random.split(key, 3)
    cols = jnp.exp(jax.random.uniform(subkeys[1], (1, D), minval=-1.15, maxval=1.15))
    rows = jnp.exp(jax.random.uniform(subkeys[0], (TOKENS, 1), minval=-1.15, maxval=1.15))
    inner = jnp.clip(jax.random.normal(subkeys[2], (TOKENS, D)), -6.0, 6.0)
    return (inner * rows * cols).astype(jnp.bfloat16)


def draw_fresh_latents(key, part):
    pull_weight = 0.0
    fresh_keys, aligned = fresh_plan(key, pull_weight)
    return fresh_keys.reshape(TOKENS, KVW).astype(jnp.bfloat16)


def draw_queries(key, part):
    pull_weight = 0.0
    fresh_keys, aligned = fresh_plan(key, pull_weight)
    key = jax.random.fold_in(key, 13)
    jitter = jnp.clip(jax.random.normal(key, (REQUESTS, 2, HEADS, KVW)), -6.0, 6.0)
    query_rows = jitter + 0.06 * fresh_keys[:, :, None, :]
    weight_on = aligned[:, :, None]
    second_row = query_rows[:, 1] * (1.0 - weight_on)
    query_rows = jnp.stack([query_rows[:, 0], second_row], 1)
    return query_rows.reshape(TOKENS, HEADS * KVW).astype(jnp.bfloat16)


def draw_prefill_owner(key, part):
    shared = owner_plan(key)
    return shared[0]


def draw_prefill_slot(key, part):
    shared = owner_plan(key)
    return shared[1]


def draw_page_lists(key, part):
    shared = page_plan(key)
    return shared[0]


def draw_context_len(key, part):
    shared = page_plan(key)
    return shared[1]


def shard_levels(rng, shape, cuts, least, high):
    loudness = 1.0
    for dim, shards_of in cuts:
        draws = jax.random.uniform(jax.random.fold_in(jax.random.fold_in(rng, 6), dim), (shards_of,), jnp.float32, least / len(cuts), high / len(cuts))
        loudness = loudness * jnp.repeat(jnp.exp(draws), shape[dim] // shards_of).reshape((-1,) + (1,) * (len(shape) - 1 - dim))
    return loudness


def noise(rng, shape, scale, most, shards=(), kind=jnp.bfloat16):
    array = jax.random.normal(rng, shape, jnp.float32) * scale
    if len(shards) > 0:
        array = shard_levels(rng, shape, shards, -0.22, 0.18) * array
    return jnp.clip(array, min=-most, max=most).astype(kind)


def setup_inputs(seed: int = 0) -> dict:
    keys = jax.random.split(jax.random.key(seed), 16)
    residual = draw_residual(jax.random.fold_in(keys[15], 71), 0)
    queries = draw_queries(jax.random.fold_in(keys[15], 71), 0)
    fresh_latents = draw_fresh_latents(jax.random.fold_in(keys[15], 71), 0)
    cache_pages = noise(keys[3], (RES_DEV * N_GRP * N_TP, PAGE * KVW), 1.0, 6.0, ((0, 128),))
    prefill_pages = noise(keys[4], (PRE_DEV * N_GRP * N_TP, PAGE * KVW), 1.0, 6.0, ((0, 128),))
    prefill_owner = draw_prefill_owner(jax.random.fold_in(keys[15], 71), 0)
    prefill_slot = draw_prefill_slot(jax.random.fold_in(keys[15], 71), 0)
    page_lists = draw_page_lists(jax.random.fold_in(keys[15], 71), 0)
    context_len = draw_context_len(jax.random.fold_in(keys[15], 71), 0)
    value_up = noise(keys[9], (HEADS, LAT, HEADV), LAT ** -0.5, 0.25, ((0, 32),))
    out_proj = noise(keys[10], (HEADS * HEADV, D), (HEADS * HEADV // 16) ** -0.5, 0.1875, ((0, 32),))
    norm_gain = jnp.clip(1.0 + 0.1 * jax.random.normal(keys[11], (D,), jnp.float32), 0.5, 1.5).astype(jnp.bfloat16)
    gate_weight = noise(keys[12], (D, FF), D ** -0.5, 0.0625, ((1, 32),))
    up_weight = noise(keys[13], (D, FF), D ** -0.5, 0.0625, ((1, 32),))
    down_weight = noise(keys[14], (FF, D), FF ** -0.5, 0.0625, ((0, 32),))
    return {"residual": residual, "queries": queries, "fresh_latents": fresh_latents, "cache_pages": cache_pages, "prefill_pages": prefill_pages, "prefill_owner": prefill_owner, "prefill_slot": prefill_slot, "page_lists": page_lists, "context_len": context_len, "value_up": value_up, "out_proj": out_proj, "norm_gain": norm_gain, "gate_weight": gate_weight, "up_weight": up_weight, "down_weight": down_weight}


def rms_norm(hidden, norm_gain):
    values = hidden.astype(jnp.float32)
    spread = lax.optimization_barrier(jnp.mean(values * values, -1, keepdims=True))
    return (values * lax.rsqrt(spread + 1e-06) * norm_gain.astype(jnp.float32)).astype(jnp.bfloat16)

def attend_request(query_rows, fresh_rows, cache_keys, length):
    scale = (HEADV + ROPE) ** (-0.5)
    query_f = query_rows.astype(jnp.float32)
    keys_f = cache_keys.astype(jnp.float32)
    fresh_f = fresh_rows.astype(jnp.float32)
    cached = jnp.einsum('jhc,kc->jhk', query_f, keys_f) * scale
    visible = jnp.arange(keys_f.shape[0], dtype=jnp.int32) < length
    cached = jnp.where(visible[None, None, :], cached, -jnp.inf)
    recent = jnp.einsum('jhc,kc->jhk', query_f, fresh_f) * scale
    causal = jnp.arange(2)[:, None] >= jnp.arange(2)[None, :]
    recent = jnp.where(causal[:, None, :], recent, -jnp.inf)
    peak = jnp.maximum(lax.optimization_barrier(jnp.max(cached, -1)), lax.optimization_barrier(jnp.max(recent, -1)))[..., None]
    cached_exp = jnp.exp(cached - peak)
    recent_exp = jnp.exp(recent - peak)
    denominator = lax.optimization_barrier(jnp.sum(cached_exp, -1, keepdims=True)) + lax.optimization_barrier(jnp.sum(recent_exp, -1, keepdims=True))
    cached_prob = lax.optimization_barrier((cached_exp / denominator).astype(jnp.bfloat16)).astype(jnp.float32)
    recent_prob = lax.optimization_barrier((recent_exp / denominator).astype(jnp.bfloat16)).astype(jnp.float32)
    mixed = jnp.einsum('jhk,kl->jhl', cached_prob, keys_f[:, :LAT]) + jnp.einsum('jhk,kl->jhl', recent_prob, fresh_f[:, :LAT])
    return mixed.astype(jnp.bfloat16)

def reference(residual, queries, fresh_latents, cache_pages, prefill_pages, prefill_owner, prefill_slot, page_lists, context_len, value_up, out_proj, norm_gain, gate_weight, up_weight, down_weight):
    devices = N_GRP * N_TP
    page_width = PAGE * KVW
    sources = jnp.arange(prefill_pages.shape[0], dtype=jnp.int32)
    column = sources // PRE_DEV % N_TP
    targets = ((prefill_owner * N_TP + column) * PRE_DEV + prefill_slot).astype(jnp.int32)
    received = jnp.zeros_like(prefill_pages).at[targets].set(prefill_pages)
    pool = jnp.concatenate([cache_pages.reshape(devices, RES_DEV, page_width), received.reshape(devices, PRE_DEV, page_width)], 1)
    pool = pool.reshape(devices * POOL, PAGE, KVW)
    query_all = queries.reshape(REQUESTS, 2, HEADS, KVW)
    fresh_all = fresh_latents.reshape(REQUESTS, 2, KVW)
    owners = jnp.arange(REQUESTS, dtype=jnp.int32) // REQ_DEV

    def per_request(items):
        query_rows, fresh_rows, page_row, length, owner = items
        cache_keys = pool[(owner * POOL + page_row).astype(jnp.int32)].reshape(MAXP * PAGE, KVW)
        return attend_request(query_rows, fresh_rows, cache_keys, length)
    attended = lax.map(per_request, (query_all, fresh_all, page_lists, context_len, owners))
    attended = attended.reshape(TOKENS, HEADS, LAT)
    values = jnp.einsum('thl,hlv->thv', attended.astype(jnp.float32), value_up.astype(jnp.float32)).astype(jnp.bfloat16)
    attn_out = jnp.dot(values.reshape(TOKENS, HEADS * HEADV), out_proj, preferred_element_type=jnp.float32)
    hidden = (residual.astype(jnp.float32) + attn_out).astype(jnp.bfloat16)
    normed = rms_norm(hidden, norm_gain)
    gate = jnp.dot(normed, gate_weight, preferred_element_type=jnp.float32)
    up_part = jnp.dot(normed, up_weight, preferred_element_type=jnp.float32)
    act = (jax.nn.silu(gate) * up_part).astype(jnp.bfloat16)
    mlp = jnp.dot(act, down_weight, preferred_element_type=jnp.float32)
    return (hidden.astype(jnp.float32) + mlp).astype(jnp.bfloat16)
```

```python
import math

import jax
import jax.numpy as jnp
from jax import lax
from jax.experimental import pallas as pl
from jax.experimental.pallas import tpu as pltpu
from jax.sharding import PartitionSpec as P

HEADS = 128
LAT = 512
ROPE = 64
HEADV = 128
PAGE = 64
KVW = 576
MOST = 8
PAGE_WIDTH = PAGE * KVW
PAIR = 2 * KVW
RES_BLOCKS = 11
UNROLL = 16
PRODUCT_WIDTH = 512
HIDDEN_WIDTH = 1792
REC_BLOCKS = 5
RES_SPARE = (RES_BLOCKS + 1) * 8
REC_SPARE = (REC_BLOCKS + 1) * 8
KEYS = 8 * PAGE
LOW = -1e30
EXPONENT = (HEADV + ROPE) ** (-0.5) * math.log2(math.e)
ROWS = 2 * HEADS
NT = (((1,), (1,)), ((), ()))
MIB = 1024 * 1024


def rms_norm(hidden, norm_gain):
    values = hidden.astype(jnp.float32)
    spread = jnp.mean(values * values, -1, keepdims=True)
    return (values * lax.rsqrt(spread + 1e-06) * norm_gain.astype(jnp.float32)).astype(jnp.bfloat16)


def chip_pairs(step0, step1):
    pairs = []
    for y in range(4):
        for x in range(4):
            for core, (dy, dx, flip) in enumerate((step0, step1)):
                there = (((y + dy) % 4) * 4 + (x + dx) % 4) * 2 + (core ^ flip)
                pairs.append(((y * 4 + x) * 2 + core, there))
    return pairs


def swap_cores(block):
    return lax.ppermute(block, "tp", chip_pairs((0, 0, 1), (0, 0, 1)))


def along_first(block, k):
    return lax.ppermute(block, "tp", chip_pairs((0, k, 0), (k, 0, 0)))


def along_second(block, k):
    return lax.ppermute(block, "tp", chip_pairs((k, 0, 0), (0, k, 0)))


def token_order():
    t = lax.axis_index("tp")
    y, x, core = t // 8, (t // 2) % 4, t % 2
    row = jnp.arange(256, dtype=jnp.int32)
    owner_core = jnp.where(row // 128 == 0, core, 1 - core)
    k1, k2, i = (row // 32) % 4, (row // 8) % 4, row % 8
    dy = jnp.where(owner_core == 0, k2, k1)
    dx = jnp.where(owner_core == 0, k1, k2)
    return ((((y + dy) % 4) * 4 + (x + dx) % 4) * 2 + owner_core) * 8 + i


def add_up(own, others):
    total = own.astype(jnp.float32)
    for other in others:
        total = total + other.astype(jnp.float32)
    return total


def reduce_rows(mine, theirs):
    got = {k: swap_cores(theirs[k]) for k in (1, 3, 2, 0)}
    chunks = {k: add_up(mine[k], [got[k]]) for k in (1, 3, 2, 0)}
    arrived = [along_first(chunks[k].astype(jnp.bfloat16), k) for k in (1, 3, 2)]
    chunks = add_up(chunks[0], arrived).reshape(4, 8, -1)
    arrived = [along_second(chunks[k].astype(jnp.bfloat16), k) for k in (1, 3, 2)]
    return add_up(chunks[0], arrived)


def gather_rows(block):
    arrived = {k: along_second(block, 4 - k) for k in (1, 3, 2)}
    rows = jnp.concatenate([block] + [arrived[k] for k in (1, 2, 3)], 0)
    arrived = {k: along_first(rows, 4 - k) for k in (1, 3, 2)}
    mine = [rows] + [arrived[k] for k in (1, 2, 3)]
    return mine + [swap_cores(part) for part in mine]


def iota(shape, dim):
    return lax.broadcasted_iota(jnp.int32, shape, dim)


def outbox_kernel(route, pages, out1, out2, out3):
    outs = (out1, out2, out3)
    rows, cols = iota((32, 128), 0), iota((32, 128), 1)
    pick = jnp.zeros((32, 128), jnp.float32)
    slots = jnp.full((32, 128), 64, jnp.int32)
    counts = [jnp.int32(0)] * 4
    for i in range(16):
        step = route[i] >> 4
        rank = jnp.int32(0)
        for k in range(1, 4):
            rank = jnp.where(step == k, counts[k], rank)
            counts[k] = counts[k] + jnp.where(step == k, 1, 0)
        target = jnp.where(step == 0, -1, (step - 1) * MOST + rank)
        pick = jnp.where((rows == target) & (cols == i), 1.0, pick)
        slots = jnp.where(rows == target, route[i] & 15, slots)
    pick = pick[:, :16].astype(jnp.bfloat16)
    slots = slots.astype(jnp.float32).astype(jnp.bfloat16)

    def chunk(n, _):
        for u in range(UNROLL):
            lanes = pl.ds(pl.multiple_of((n * UNROLL + u) * PAIR, 128), PAIR)
            got = jnp.dot(pick, pages[:, lanes], preferred_element_type=jnp.float32)
            for k in range(3):
                outs[k][:, lanes] = got[k * 8 : k * 8 + 8].astype(jnp.bfloat16)
        return 0

    lax.fori_loop(0, PAGE // 2 // UNROLL, chunk, 0)
    for k in range(3):
        outs[k][:, PAGE_WIDTH:] = slots[k * 8 : k * 8 + 8]


def outbox(route, pages):
    smem, vmem = pl.BlockSpec(memory_space=pltpu.SMEM), pl.BlockSpec(memory_space=pltpu.VMEM)
    return pl.pallas_call(
        outbox_kernel,
        out_shape=[jax.ShapeDtypeStruct((MOST, PAGE_WIDTH + 128), jnp.bfloat16)] * 3,
        in_specs=[smem, vmem],
        out_specs=[vmem] * 3,
        compiler_params=pltpu.CompilerParams(vmem_limit_bytes=16 * MIB),
        name="outbox",
    )(route, pages)


def lay_keys(pick, source, keys, blocks):
    def chunk(n, _):
        for u in range(UNROLL):
            at = n * UNROLL + u
            lanes = pl.ds(pl.multiple_of(at * PAIR, 128), PAIR)
            got = jnp.dot(pick, source(lanes), preferred_element_type=jnp.float32)
            even = got[: blocks * 8, :KVW].reshape(blocks, 8, KVW)
            odd = got[: blocks * 8, KVW:].reshape(blocks, 8, KVW)
            both = jnp.concatenate([even, odd], 1).astype(jnp.bfloat16)
            keys[:, pl.ds(pl.multiple_of(at * 16, 16), 16), :] = both
        return 0

    lax.fori_loop(0, PAGE // 2 // UNROLL, chunk, 0)


def key_limit(first, valid):
    at = iota((8, KEYS), 1)
    limit = jnp.zeros((8, KEYS), jnp.int32)
    for i in range(8):
        limit = jnp.where((at & 7) == i, valid[first + i], limit)
    return ((at >> 3) < limit)[:1]


def absorb(scores, live, value_rows, peak, total, acc, r):
    scores = jnp.where(live, scores * EXPONENT, LOW)
    before = peak[r]
    top = jnp.maximum(before, jnp.max(scores, -1, keepdims=True))
    weight = jnp.exp2(scores - top[:, :1])
    fade = jnp.exp2(before - top)
    peak[r] = top
    total[r] = total[r] * fade + jnp.sum(weight, -1, keepdims=True)
    acc[r] = acc[r] * fade[:, :1] + jnp.dot(
        weight.astype(jnp.bfloat16), value_rows, preferred_element_type=jnp.float32
    )


def absorb_blocks(blocks, first, valid, query_rows, keys, peak, total, acc, even, odd):
    def request_of(b):
        r = jnp.int32(0)
        for n in range(1, 4):
            r = r + jnp.where(b >= first[n], 1, 0)
        return r

    def scores_of(b):
        return lax.dot_general(
            query_rows[request_of(b)], keys[jnp.minimum(b, blocks - 1)], NT, preferred_element_type=jnp.float32
        )

    def take(b, scores):
        value_rows = keys[jnp.minimum(b, blocks - 1), :, :LAT]
        absorb(scores[...], key_limit(b * 8, valid), value_rows, peak, total, acc, request_of(b))

    even[...] = scores_of(0)

    def step(n, _):
        odd[...] = scores_of(2 * n + 1)
        take(2 * n, even)
        even[...] = scores_of(2 * n + 2)
        take(2 * n + 1, odd)
        return 0

    lax.fori_loop(0, (first[4] + 1) // 2, step, 0)


def resident_kernel(
    lists, lengths, queries, fresh, cache,
    query_rows, peak, total, acc, slot_row, rec_valid, rec_first,
    keys, even, odd, head_rows, res_page, res_valid, res_first,
):
    for i in range(RES_BLOCKS * 8):
        res_page[i] = 0
    for i in range(RES_SPARE):
        res_valid[i] = 0
    for i in range(REC_SPARE):
        rec_valid[i] = 0
    for i in range(17):
        slot_row[i] = 0
    res_at, rec_at = jnp.int32(0), jnp.int32(0)
    for r in range(4):
        res_first[r] = res_at // 8
        rec_first[r] = rec_at // 8
        length = lengths[r]

        def page(p, carry):
            res_at, rec_at = carry
            entry = lists[r, p]
            live = jnp.minimum(length - p * PAGE, PAGE)
            resident = entry < 64
            at = jnp.where(resident, res_at, RES_SPARE)
            res_page[at] = entry
            res_valid[at] = live
            at = jnp.where(resident, REC_SPARE, rec_at)
            rec_valid[at] = live
            slot_row[jnp.where(resident, 16, entry - 64)] = rec_at
            one = jnp.where(resident, 1, 0)
            return res_at + one, rec_at + 1 - one

        res_at, rec_at = lax.fori_loop(0, (length + PAGE - 1) // PAGE, page, (res_at, rec_at))
        res_at = (res_at + 7) // 8 * 8
        rec_at = (rec_at + 7) // 8 * 8
    res_first[4] = res_at // 8
    rec_first[4] = rec_at // 8

    to, of = iota((128, 128), 0), iota((128, 128), 1)
    wanted = ((to >> 1) & 15) * 8 + (to >> 5) * 2 + (to & 1)
    order = (wanted == of).astype(jnp.float32).astype(jnp.bfloat16)
    for g in range(HEADS // 16):
        for n in range(8):
            two = queries[:, (g * 8 + n) * PAIR : (g * 8 + n + 1) * PAIR].astype(jnp.float32)
            head_rows[pl.ds(n * 16, 16), :] = jnp.concatenate(
                [two[:, :KVW], two[:, KVW:]], 0
            ).astype(jnp.bfloat16)
        placed = jnp.dot(order, head_rows[...], preferred_element_type=jnp.float32).astype(jnp.bfloat16)
        for r in range(4):
            query_rows[r, g * 32 : g * 32 + 32, :] = placed[r * 32 : r * 32 + 32]

    new_keys = jnp.concatenate([fresh[...].astype(jnp.float32), jnp.zeros((120, KVW), jnp.float32)], 0).astype(jnp.bfloat16)
    for r in range(4):
        scores = lax.dot_general(query_rows[r], new_keys, NT, preferred_element_type=jnp.float32) * EXPONENT
        column, j = iota((ROWS, 128), 1), iota((ROWS, 128), 0) & 1
        seen = (column == 2 * r) | ((column == 2 * r + 1) & (j == 1))
        scores = jnp.where(seen, scores, LOW)
        top = jnp.max(scores, -1, keepdims=True)
        weight = jnp.exp2(scores - top)
        peak[r] = jnp.broadcast_to(top, (ROWS, 128))
        total[r] = jnp.broadcast_to(jnp.sum(weight, -1, keepdims=True), (ROWS, 128))
        acc[r] = jnp.dot(weight.astype(jnp.bfloat16), new_keys[:, :LAT], preferred_element_type=jnp.float32)

    pick = []
    sub, lane = iota((8, 64), 0), iota((8, 64), 1)
    for b in range(RES_BLOCKS):
        source = jnp.zeros((8, 64), jnp.int32)
        for i in range(8):
            source = jnp.where(sub == i, res_page[b * 8 + i], source)
        pick.append((source == lane).astype(jnp.float32))
    pick.append(jnp.zeros((8, 64), jnp.float32))
    pick = jnp.concatenate(pick, 0).astype(jnp.bfloat16)
    lay_keys(pick, lambda lanes: cache[:, lanes], keys, RES_BLOCKS)

    absorb_blocks(RES_BLOCKS, res_first, res_valid, query_rows, keys, peak, total, acc, even, odd)


def attend_resident(lists, lengths, queries, fresh, cache):
    smem, vmem = pl.BlockSpec(memory_space=pltpu.SMEM), pl.BlockSpec(memory_space=pltpu.VMEM)
    shapes = [
        jax.ShapeDtypeStruct((4, ROWS, KVW), jnp.bfloat16),
        jax.ShapeDtypeStruct((4, ROWS, 128), jnp.float32),
        jax.ShapeDtypeStruct((4, ROWS, 128), jnp.float32),
        jax.ShapeDtypeStruct((4, ROWS, LAT), jnp.float32),
        jax.ShapeDtypeStruct((24,), jnp.int32),
        jax.ShapeDtypeStruct((REC_SPARE + 8,), jnp.int32),
        jax.ShapeDtypeStruct((8,), jnp.int32),
    ]
    return pl.pallas_call(
        resident_kernel,
        out_shape=shapes,
        in_specs=[smem, smem, vmem, vmem, vmem],
        out_specs=[vmem] * 4 + [smem] * 3,
        scratch_shapes=[
            pltpu.VMEM((RES_BLOCKS, KEYS, KVW), jnp.bfloat16),
            pltpu.VMEM((ROWS, KEYS), jnp.float32),
            pltpu.VMEM((ROWS, KEYS), jnp.float32),
            pltpu.VMEM((128, KVW), jnp.bfloat16),
            pltpu.SMEM((RES_SPARE + 8,), jnp.int32),
            pltpu.SMEM((RES_SPARE + 8,), jnp.int32),
            pltpu.SMEM((8,), jnp.int32),
        ],
        compiler_params=pltpu.CompilerParams(vmem_limit_bytes=20 * MIB),
        cost_estimate=pl.CostEstimate(flops=8_000_000_000, bytes_accessed=12_000_000, transcendentals=2_000_000),
        name="attend_resident",
    )(lists, lengths, queries, fresh, cache)


def received_kernel(
    route, slot_row, rec_valid, rec_first,
    box1, box2, box3, own, query_rows, peak_in, total_in, acc_in,
    out, keys, even, odd, peak, total, acc,
):
    peak[...] = peak_in[...]
    total[...] = total_in[...]
    acc[...] = acc_in[...]
    boxes = (box1, box2, box3)
    cols = iota((24, 128), 1)
    slots = jnp.concatenate([box[:, PAGE_WIDTH:].astype(jnp.float32) for box in boxes], 0)
    arrived = jnp.zeros((24, 128), jnp.float32)
    for n in range(16):
        arrived = jnp.where((slots == float(n)) & (cols == slot_row[n]), 1.0, arrived)
    rows, cols = iota((16, 128), 0), iota((16, 128), 1)
    kept = jnp.zeros((16, 128), jnp.float32)
    for i in range(16):
        target = jnp.where(route[i] >> 4 == 0, slot_row[route[i] & 15], -1)
        kept = jnp.where((rows == i) & (cols == target), 1.0, kept)
    place_of = jnp.concatenate([arrived, kept, jnp.zeros((88, 128), jnp.float32)], 0)
    pick = place_of.T[:48, :48].astype(jnp.bfloat16)

    def source(lanes):
        parts = [box[:, lanes].astype(jnp.float32) for box in boxes]
        parts.append(own[:, lanes].astype(jnp.float32))
        parts.append(jnp.zeros((8, PAIR), jnp.float32))
        return jnp.concatenate(parts, 0).astype(jnp.bfloat16)

    lay_keys(pick, source, keys, REC_BLOCKS)

    absorb_blocks(REC_BLOCKS, rec_first, rec_valid, query_rows, keys, peak, total, acc, even, odd)
    for t in range(0, 32, 8):
        parts = []
        for r in range(4):
            part = acc[r, t * 8 : t * 8 + 64] * (1.0 / total[r, t * 8 : t * 8 + 64, :1])
            parts.append(part.reshape(8, 8, LAT))
        out[t : t + 8] = jnp.concatenate(parts, 1).astype(jnp.bfloat16)


def attend_received(route, plan, boxes, own, state):
    smem, vmem = pl.BlockSpec(memory_space=pltpu.SMEM), pl.BlockSpec(memory_space=pltpu.VMEM)
    return pl.pallas_call(
        received_kernel,
        out_shape=jax.ShapeDtypeStruct((32, 32, LAT), jnp.bfloat16),
        in_specs=[smem] * 4 + [vmem] * 8,
        out_specs=vmem,
        scratch_shapes=[
            pltpu.VMEM((REC_BLOCKS, KEYS, KVW), jnp.bfloat16),
            pltpu.VMEM((ROWS, KEYS), jnp.float32),
            pltpu.VMEM((ROWS, KEYS), jnp.float32),
            pltpu.VMEM((4, ROWS, 128), jnp.float32),
            pltpu.VMEM((4, ROWS, 128), jnp.float32),
            pltpu.VMEM((4, ROWS, LAT), jnp.float32),
        ],
        compiler_params=pltpu.CompilerParams(vmem_limit_bytes=20 * MIB),
        name="attend_received",
    )(route, *plan, *boxes, own, *state)


def product(rows, weight, store):
    width = PRODUCT_WIDTH

    def part(n, _):
        lanes = pl.ds(pl.multiple_of(n * width, 128), width)
        store(lanes, jnp.dot(rows, weight[:, lanes], preferred_element_type=jnp.float32))
        return 0

    lax.fori_loop(0, weight.shape[1] // width, part, 0, unroll=True)


def store_blocks(outs):
    def store(lanes, got):
        for k, out in enumerate(outs):
            out[:, lanes] = got[k * 32 : k * 32 + 32].astype(jnp.bfloat16)

    return store


def values_kernel(order, rows, value_up, out_proj, values_out, *theirs):
    wide = jnp.concatenate([value_up[h] for h in range(4)], 1)
    all_heads = jnp.dot(rows[...], wide, preferred_element_type=jnp.float32)
    at, column = iota((1024, 512), 0), iota((1024, 512), 1)
    own_head = ((at >> 1) & 3) == (column >> 7)
    values = jnp.where(own_head, all_heads, 0.0).astype(jnp.bfloat16)
    n = iota((256, 1024), 1)
    token = (n >> 5) * 8 + ((n >> 3) & 3) * 2 + (n & 1)
    pick = (order[...] == token).astype(jnp.float32).astype(jnp.bfloat16)
    values = jnp.dot(pick, values, preferred_element_type=jnp.float32).astype(jnp.bfloat16)
    values_out[...] = values[:128]
    product(values[128:], out_proj, store_blocks(theirs))


def project_values(order, rows, value_up, out_proj):
    vmem = pl.BlockSpec(memory_space=pltpu.VMEM)
    width = out_proj.shape[1]
    return pl.pallas_call(
        values_kernel,
        out_shape=[jax.ShapeDtypeStruct((128, 512), jnp.bfloat16)]
        + [jax.ShapeDtypeStruct((32, width), jnp.bfloat16)] * 4,
        in_specs=[vmem] * 4,
        out_specs=[vmem] * 5,
        compiler_params=pltpu.CompilerParams(vmem_limit_bytes=20 * MIB),
        cost_estimate=pl.CostEstimate(flops=2_500_000_000, bytes_accessed=12_000_000, transcendentals=0),
        name="values",
    )(order, rows, value_up, out_proj)


def project_kernel(rows, weight, *outs):
    def store(lanes, got):
        for k, out in enumerate(outs):
            out[:, lanes] = got[k * 32 : k * 32 + 32]

    product(rows[...], weight, store)


def project(rows, weight):
    vmem = pl.BlockSpec(memory_space=pltpu.VMEM)
    width = weight.shape[1]
    return pl.pallas_call(
        project_kernel,
        out_shape=[jax.ShapeDtypeStruct((32, width), jnp.float32)] * 4,
        in_specs=[vmem] * 2,
        out_specs=[vmem] * 4,
        compiler_params=pltpu.CompilerParams(vmem_limit_bytes=16 * MIB),
        cost_estimate=pl.CostEstimate(flops=1_000_000_000, bytes_accessed=11_000_000, transcendentals=0),
        name="project",
    )(rows, weight)


def hidden_kernel(*refs):
    rows, (gate_weight, up_weight, down_weight, act_out), theirs = refs[:8], refs[8:12], refs[12:16]
    gate, up_part = refs[16:]
    width = HIDDEN_WIDTH
    for n in range(rows[0].shape[1] // width):
        lanes = slice(n * width, n * width + width)
        block = jnp.concatenate([row[:, lanes] for row in rows], 0)
        for total, weight in ((gate, gate_weight), (up_part, up_weight)):
            got = lax.dot_general(weight[:, lanes], block, NT, preferred_element_type=jnp.float32)
            total[...] = got if n == 0 else total[...] + got
    g = gate[...]
    act = (g / (1.0 + jnp.exp(-g)) * up_part[...]).T.astype(jnp.bfloat16)
    act_out[...] = act[:128]
    product(act[128:], down_weight, store_blocks(theirs))


def hidden_units(rows, gate_weight, up_weight, down_weight):
    vmem = pl.BlockSpec(memory_space=pltpu.VMEM)
    units, width = down_weight.shape
    return pl.pallas_call(
        hidden_kernel,
        out_shape=[jax.ShapeDtypeStruct((128, units), jnp.bfloat16)]
        + [jax.ShapeDtypeStruct((32, width), jnp.bfloat16)] * 4,
        in_specs=[vmem] * 11,
        out_specs=[vmem] * 5,
        scratch_shapes=[pltpu.VMEM((units, 256), jnp.float32)] * 2,
        compiler_params=pltpu.CompilerParams(vmem_limit_bytes=20 * MIB),
        cost_estimate=pl.CostEstimate(flops=3_000_000_000, bytes_accessed=18_000_000, transcendentals=80_000),
        name="hidden_units",
    )(*rows, gate_weight.T, up_weight.T, down_weight)


def shards(
    residual,
    queries,
    fresh_latents,
    cache_pages,
    prefill_pages,
    prefill_owner,
    prefill_slot,
    page_lists,
    context_len,
    value_up,
    out_proj,
    norm_gain,
    gate_weight,
    up_weight,
    down_weight,
):
    route = ((prefill_owner - lax.axis_index("grp")) & 3) * 16 + prefill_slot
    boxes = outbox(route, prefill_pages)
    boxes = [
        lax.ppermute(box, "grp", [(g, (g + k) % 4) for g in range(4)])
        for k, box in enumerate(boxes, 1)
    ]
    *state, slot_row, rec_valid, rec_first = attend_resident(
        page_lists, context_len, queries, fresh_latents, cache_pages
    )
    attended = attend_received(
        route, (slot_row, rec_valid, rec_first), boxes, prefill_pages, state
    )
    by_heads = lax.all_to_all(attended, "tp", split_axis=0, concat_axis=0, tiled=True)
    values, *theirs = project_values(token_order()[:, None], by_heads.reshape(1024, LAT), value_up, out_proj)
    attn_out = reduce_rows(project(values, out_proj), theirs)
    hidden = (residual.astype(jnp.float32) + attn_out).astype(jnp.bfloat16)
    normed = rms_norm(hidden, norm_gain)
    act, *theirs = hidden_units(gather_rows(normed), gate_weight, up_weight, down_weight)
    mlp = reduce_rows(project(act, down_weight), theirs)
    return (hidden.astype(jnp.float32) + mlp).astype(jnp.bfloat16)


def solution(mesh):
    placed = (
        P(("grp", "tp"), None),
        P(("grp", "tp"), None),
        P(("grp", "tp"), None),
        P(("grp", "tp"), None),
        P(("grp", "tp"), None),
        P(("grp", "tp")),
        P(("grp", "tp")),
        P(("grp", "tp"), None),
        P(("grp", "tp")),
        P("tp", None, None),
        P("tp", None),
        P(),
        P(None, "tp"),
        P(None, "tp"),
        P("tp", None),
    )
    return jax.shard_map(
        shards, mesh=mesh, in_specs=placed, out_specs=P(("grp", "tp"), None), check_vma=False
    )
```

```python
import math

import jax
import jax.numpy as jnp
from jax import lax
from jax.experimental import pallas as pl
from jax.experimental.pallas import tpu as pltpu
from jax.sharding import PartitionSpec as P

HEADS = 128
LAT = 512
ROPE = 64
HEADV = 128
PAGE = 64
KVW = 576
MOST = 8
PAGE_WIDTH = PAGE * KVW
PAIR = 2 * KVW
RES_BLOCKS = 11
UNROLL = 16
PRODUCT_WIDTH = 512
HIDDEN_WIDTH = 1792
REC_BLOCKS = 5
RES_SPARE = (RES_BLOCKS + 1) * 8
REC_SPARE = (REC_BLOCKS + 1) * 8
KEYS = 8 * PAGE
LOW = -1e30
EXPONENT = (HEADV + ROPE) ** (-0.5) * math.log2(math.e)
ROWS = 2 * HEADS
NT = (((1,), (1,)), ((), ()))
MIB = 1024 * 1024


def chip_pairs(step0, step1):
    pairs = []
    for y in range(4):
        for x in range(4):
            for core, (dy, dx, flip) in enumerate((step0, step1)):
                there = (((y + dy) % 4) * 4 + (x + dx) % 4) * 2 + (core ^ flip)
                pairs.append(((y * 4 + x) * 2 + core, there))
    return pairs


def swap_cores(block):
    return lax.ppermute(block, "tp", chip_pairs((0, 0, 1), (0, 0, 1)))


def along_first(block, k):
    return lax.ppermute(block, "tp", chip_pairs((0, k, 0), (k, 0, 0)))


def along_second(block, k):
    return lax.ppermute(block, "tp", chip_pairs((k, 0, 0), (0, k, 0)))


def token_order():
    t = lax.axis_index("tp")
    y, x, core = t // 8, (t // 2) % 4, t % 2
    row = jnp.arange(256, dtype=jnp.int32)
    owner_core = jnp.where(row // 128 == 0, core, 1 - core)
    k1, k2, i = (row // 32) % 4, (row // 8) % 4, row % 8
    dy = jnp.where(owner_core == 0, k2, k1)
    dx = jnp.where(owner_core == 0, k1, k2)
    return ((((y + dy) % 4) * 4 + (x + dx) % 4) * 2 + owner_core) * 8 + i


def add_up(own, others):
    total = own.astype(jnp.float32)
    for other in others:
        total = total + other.astype(jnp.float32)
    return total


def reduce_first(mine, theirs):
    got = {k: swap_cores(theirs[k]) for k in (1, 3, 2, 0)}
    chunks = {k: add_up(mine[k], [got[k]]).astype(jnp.bfloat16) for k in (1, 3, 2)}
    return [mine[0], got[0]] + [along_first(chunks[k], k) for k in (1, 3, 2)]


def reduce_second(terms):
    chunks = add_up(terms[0], terms[1:]).reshape(4, 8, -1)
    arrived = [along_second(chunks[k].astype(jnp.bfloat16), k) for k in (1, 3, 2)]
    return add_up(chunks[0], arrived)


def share_kernel(residual, *refs):
    terms, (total, sent) = refs[:-2], refs[-2:]
    for n in range(0, total.shape[1], 1024):
        lanes = slice(n, n + 1024)
        own = terms[0][:, lanes]
        for term in terms[1:]:
            own = own + term[:, lanes].astype(jnp.float32)
        first = own[:8] + residual[:, lanes].astype(jnp.float32)
        own = jnp.concatenate([first, own[8:]], 0)
        total[:, lanes] = own
        sent[:, lanes] = own.astype(jnp.bfloat16)


def settle_kernel(total, got1, got2, got3, norm_gain, hidden_out, normed, hidden):
    width = total.shape[1]
    squares = jnp.zeros((32, 1), jnp.float32)
    for n in range(0, width, 1024):
        lanes = slice(n, n + 1024)
        block = total[:, lanes]
        for k, got in ((1, got1), (2, got2), (3, got3)):
            got = got[:, lanes].astype(jnp.float32)
            block = block + jnp.concatenate([got[k * 8 :], got[: k * 8]], 0)
        block = block.astype(jnp.bfloat16)
        hidden_out[:, lanes] = block[:8]
        block = block.astype(jnp.float32)
        hidden[:, lanes] = block
        squares = squares + jnp.sum(block * block, -1, keepdims=True)
    spread = lax.rsqrt(squares * (1.0 / width) + 1e-06)
    for n in range(0, width, 1024):
        lanes = slice(n, n + 1024)
        gain = norm_gain[:, lanes].astype(jnp.float32)
        normed[:, lanes] = (hidden[:, lanes] * spread * gain).astype(jnp.bfloat16)


def settle(terms, residual, norm_gain):
    vmem = pl.BlockSpec(memory_space=pltpu.VMEM)
    params = pltpu.CompilerParams(vmem_limit_bytes=12 * MIB)
    shape = terms[0].shape
    total, sent = pl.pallas_call(
        share_kernel,
        out_shape=[jax.ShapeDtypeStruct(shape, jnp.float32), jax.ShapeDtypeStruct(shape, jnp.bfloat16)],
        in_specs=[vmem] * 6,
        out_specs=[vmem] * 2,
        compiler_params=params,
        name="share",
    )(residual, *terms)
    got = {k: along_second(sent, k) for k in (1, 3, 2)}
    return pl.pallas_call(
        settle_kernel,
        out_shape=[
            jax.ShapeDtypeStruct(residual.shape, jnp.bfloat16),
            jax.ShapeDtypeStruct(shape, jnp.bfloat16),
        ],
        in_specs=[vmem] * 5,
        out_specs=[vmem] * 2,
        scratch_shapes=[pltpu.VMEM(shape, jnp.float32)],
        compiler_params=params,
        name="settle",
    )(total, got[1], got[2], got[3], norm_gain[None, :])


def gather_first(rows):
    arrived = {k: along_first(rows, 4 - k) for k in (1, 3, 2)}
    mine = [rows] + [arrived[k] for k in (1, 2, 3)]
    return mine + [swap_cores(part) for part in mine]


def iota(shape, dim):
    return lax.broadcasted_iota(jnp.int32, shape, dim)


def outbox_kernel(route, pages, out1, out2, out3):
    outs = (out1, out2, out3)
    rows, cols = iota((32, 128), 0), iota((32, 128), 1)
    pick = jnp.zeros((32, 128), jnp.float32)
    slots = jnp.full((32, 128), 64, jnp.int32)
    counts = [jnp.int32(0)] * 4
    for i in range(16):
        step = route[i] >> 4
        rank = jnp.int32(0)
        for k in range(1, 4):
            rank = jnp.where(step == k, counts[k], rank)
            counts[k] = counts[k] + jnp.where(step == k, 1, 0)
        target = jnp.where(step == 0, -1, (step - 1) * MOST + rank)
        pick = jnp.where((rows == target) & (cols == i), 1.0, pick)
        slots = jnp.where(rows == target, route[i] & 15, slots)
    pick = pick[:, :16].astype(jnp.bfloat16)
    slots = slots.astype(jnp.float32).astype(jnp.bfloat16)

    def chunk(n, _):
        for u in range(UNROLL):
            lanes = pl.ds(pl.multiple_of((n * UNROLL + u) * PAIR, 128), PAIR)
            got = jnp.dot(pick, pages[:, lanes], preferred_element_type=jnp.float32)
            for k in range(3):
                outs[k][:, lanes] = got[k * 8 : k * 8 + 8].astype(jnp.bfloat16)
        return 0

    lax.fori_loop(0, PAGE // 2 // UNROLL, chunk, 0)
    for k in range(3):
        outs[k][:, PAGE_WIDTH:] = slots[k * 8 : k * 8 + 8]


def outbox(route, pages):
    smem, vmem = pl.BlockSpec(memory_space=pltpu.SMEM), pl.BlockSpec(memory_space=pltpu.VMEM)
    return pl.pallas_call(
        outbox_kernel,
        out_shape=[jax.ShapeDtypeStruct((MOST, PAGE_WIDTH + 128), jnp.bfloat16)] * 3,
        in_specs=[smem, vmem],
        out_specs=[vmem] * 3,
        compiler_params=pltpu.CompilerParams(vmem_limit_bytes=16 * MIB),
        name="outbox",
    )(route, pages)


def lay_keys(pick, source, keys, blocks):
    def chunk(n, _):
        for u in range(UNROLL):
            at = n * UNROLL + u
            lanes = pl.ds(pl.multiple_of(at * PAIR, 128), PAIR)
            got = jnp.dot(pick, source(lanes), preferred_element_type=jnp.float32)
            even = got[: blocks * 8, :KVW].reshape(blocks, 8, KVW)
            odd = got[: blocks * 8, KVW:].reshape(blocks, 8, KVW)
            both = jnp.concatenate([even, odd], 1).astype(jnp.bfloat16)
            keys[:, pl.ds(pl.multiple_of(at * 16, 16), 16), :] = both
        return 0

    lax.fori_loop(0, PAGE // 2 // UNROLL, chunk, 0)


def key_limit(first, valid):
    at = iota((8, KEYS), 1)
    limit = jnp.zeros((8, KEYS), jnp.int32)
    for i in range(8):
        limit = jnp.where((at & 7) == i, valid[first + i], limit)
    return ((at >> 3) < limit)[:1]


def absorb(scores, live, value_rows, peak, total, acc, r):
    scores = jnp.where(live, scores * EXPONENT, LOW)
    before = peak[r]
    top = jnp.maximum(before, jnp.max(scores, -1, keepdims=True))
    weight = jnp.exp2(scores - top[:, :1])
    fade = jnp.exp2(before - top)
    peak[r] = top
    total[r] = total[r] * fade + jnp.sum(weight, -1, keepdims=True)
    acc[r] = acc[r] * fade[:, :1] + jnp.dot(
        weight.astype(jnp.bfloat16), value_rows, preferred_element_type=jnp.float32
    )


def absorb_blocks(blocks, first, valid, query_rows, keys, peak, total, acc, even, odd):
    def request_of(b):
        r = jnp.int32(0)
        for n in range(1, 4):
            r = r + jnp.where(b >= first[n], 1, 0)
        return r

    def scores_of(b):
        return lax.dot_general(
            query_rows[request_of(b)], keys[jnp.minimum(b, blocks - 1)], NT, preferred_element_type=jnp.float32
        )

    def take(b, scores):
        value_rows = keys[jnp.minimum(b, blocks - 1), :, :LAT]
        absorb(scores[...], key_limit(b * 8, valid), value_rows, peak, total, acc, request_of(b))

    even[...] = scores_of(0)

    def step(n, _):
        odd[...] = scores_of(2 * n + 1)
        take(2 * n, even)
        even[...] = scores_of(2 * n + 2)
        take(2 * n + 1, odd)
        return 0

    lax.fori_loop(0, (first[4] + 1) // 2, step, 0)


def resident_kernel(
    lists, lengths, queries, fresh, cache, out_proj,
    query_rows, peak, total, acc, slot_row, rec_valid, rec_first, staged,
    keys, even, odd, head_rows, res_page, res_valid, res_first, sem,
):
    staging = pltpu.make_async_copy(out_proj, staged, sem)
    staging.start()
    for i in range(RES_BLOCKS * 8):
        res_page[i] = 0
    for i in range(RES_SPARE):
        res_valid[i] = 0
    for i in range(REC_SPARE):
        rec_valid[i] = 0
    for i in range(17):
        slot_row[i] = 0
    res_at, rec_at = jnp.int32(0), jnp.int32(0)
    for r in range(4):
        res_first[r] = res_at // 8
        rec_first[r] = rec_at // 8
        length = lengths[r]

        def page(p, carry):
            res_at, rec_at = carry
            entry = lists[r, p]
            live = jnp.minimum(length - p * PAGE, PAGE)
            resident = entry < 64
            at = jnp.where(resident, res_at, RES_SPARE)
            res_page[at] = entry
            res_valid[at] = live
            at = jnp.where(resident, REC_SPARE, rec_at)
            rec_valid[at] = live
            slot_row[jnp.where(resident, 16, entry - 64)] = rec_at
            one = jnp.where(resident, 1, 0)
            return res_at + one, rec_at + 1 - one

        res_at, rec_at = lax.fori_loop(0, (length + PAGE - 1) // PAGE, page, (res_at, rec_at))
        res_at = (res_at + 7) // 8 * 8
        rec_at = (rec_at + 7) // 8 * 8
    res_first[4] = res_at // 8
    rec_first[4] = rec_at // 8

    to, of = iota((128, 128), 0), iota((128, 128), 1)
    wanted = ((to >> 1) & 15) * 8 + (to >> 5) * 2 + (to & 1)
    order = (wanted == of).astype(jnp.float32).astype(jnp.bfloat16)
    for g in range(HEADS // 16):
        for n in range(8):
            two = queries[:, (g * 8 + n) * PAIR : (g * 8 + n + 1) * PAIR].astype(jnp.float32)
            head_rows[pl.ds(n * 16, 16), :] = jnp.concatenate(
                [two[:, :KVW], two[:, KVW:]], 0
            ).astype(jnp.bfloat16)
        placed = jnp.dot(order, head_rows[...], preferred_element_type=jnp.float32).astype(jnp.bfloat16)
        for r in range(4):
            query_rows[r, g * 32 : g * 32 + 32, :] = placed[r * 32 : r * 32 + 32]

    new_keys = jnp.concatenate([fresh[...].astype(jnp.float32), jnp.zeros((120, KVW), jnp.float32)], 0).astype(jnp.bfloat16)
    for r in range(4):
        scores = lax.dot_general(query_rows[r], new_keys, NT, preferred_element_type=jnp.float32) * EXPONENT
        column, j = iota((ROWS, 128), 1), iota((ROWS, 128), 0) & 1
        seen = (column == 2 * r) | ((column == 2 * r + 1) & (j == 1))
        scores = jnp.where(seen, scores, LOW)
        top = jnp.max(scores, -1, keepdims=True)
        weight = jnp.exp2(scores - top)
        peak[r] = jnp.broadcast_to(top, (ROWS, 128))
        total[r] = jnp.broadcast_to(jnp.sum(weight, -1, keepdims=True), (ROWS, 128))
        acc[r] = jnp.dot(weight.astype(jnp.bfloat16), new_keys[:, :LAT], preferred_element_type=jnp.float32)

    pick = []
    sub, lane = iota((8, 64), 0), iota((8, 64), 1)
    for b in range(RES_BLOCKS):
        source = jnp.zeros((8, 64), jnp.int32)
        for i in range(8):
            source = jnp.where(sub == i, res_page[b * 8 + i], source)
        pick.append((source == lane).astype(jnp.float32))
    pick.append(jnp.zeros((8, 64), jnp.float32))
    pick = jnp.concatenate(pick, 0).astype(jnp.bfloat16)
    lay_keys(pick, lambda lanes: cache[:, lanes], keys, RES_BLOCKS)

    absorb_blocks(RES_BLOCKS, res_first, res_valid, query_rows, keys, peak, total, acc, even, odd)
    staging.wait()


def attend_resident(lists, lengths, queries, fresh, cache, out_proj):
    smem, vmem = pl.BlockSpec(memory_space=pltpu.SMEM), pl.BlockSpec(memory_space=pltpu.VMEM)
    shapes = [
        jax.ShapeDtypeStruct((4, ROWS, KVW), jnp.bfloat16),
        jax.ShapeDtypeStruct((4, ROWS, 128), jnp.float32),
        jax.ShapeDtypeStruct((4, ROWS, 128), jnp.float32),
        jax.ShapeDtypeStruct((4, ROWS, LAT), jnp.float32),
        jax.ShapeDtypeStruct((24,), jnp.int32),
        jax.ShapeDtypeStruct((REC_SPARE + 8,), jnp.int32),
        jax.ShapeDtypeStruct((8,), jnp.int32),
        jax.ShapeDtypeStruct(out_proj.shape, out_proj.dtype),
    ]
    return pl.pallas_call(
        resident_kernel,
        out_shape=shapes,
        in_specs=[smem, smem, vmem, vmem, vmem, pl.BlockSpec(memory_space=pl.ANY)],
        out_specs=[vmem] * 4 + [smem] * 3 + [vmem],
        scratch_shapes=[
            pltpu.VMEM((RES_BLOCKS, KEYS, KVW), jnp.bfloat16),
            pltpu.VMEM((ROWS, KEYS), jnp.float32),
            pltpu.VMEM((ROWS, KEYS), jnp.float32),
            pltpu.VMEM((128, KVW), jnp.bfloat16),
            pltpu.SMEM((RES_SPARE + 8,), jnp.int32),
            pltpu.SMEM((RES_SPARE + 8,), jnp.int32),
            pltpu.SMEM((8,), jnp.int32),
            pltpu.SemaphoreType.DMA,
        ],
        compiler_params=pltpu.CompilerParams(vmem_limit_bytes=20 * MIB),
        cost_estimate=pl.CostEstimate(flops=8_000_000_000, bytes_accessed=12_000_000, transcendentals=2_000_000),
        name="attend_resident",
    )(lists, lengths, queries, fresh, cache, out_proj)


def received_kernel(
    route, slot_row, rec_valid, rec_first,
    box1, box2, box3, own, query_rows, peak_in, total_in, acc_in,
    out, keys, even, odd, peak, total, acc,
):
    peak[...] = peak_in[...]
    total[...] = total_in[...]
    acc[...] = acc_in[...]
    boxes = (box1, box2, box3)
    cols = iota((24, 128), 1)
    slots = jnp.concatenate([box[:, PAGE_WIDTH:].astype(jnp.float32) for box in boxes], 0)
    arrived = jnp.zeros((24, 128), jnp.float32)
    for n in range(16):
        arrived = jnp.where((slots == float(n)) & (cols == slot_row[n]), 1.0, arrived)
    rows, cols = iota((16, 128), 0), iota((16, 128), 1)
    kept = jnp.zeros((16, 128), jnp.float32)
    for i in range(16):
        target = jnp.where(route[i] >> 4 == 0, slot_row[route[i] & 15], -1)
        kept = jnp.where((rows == i) & (cols == target), 1.0, kept)
    place_of = jnp.concatenate([arrived, kept, jnp.zeros((88, 128), jnp.float32)], 0)
    pick = place_of.T[:48, :48].astype(jnp.bfloat16)

    def source(lanes):
        parts = [box[:, lanes].astype(jnp.float32) for box in boxes]
        parts.append(own[:, lanes].astype(jnp.float32))
        parts.append(jnp.zeros((8, PAIR), jnp.float32))
        return jnp.concatenate(parts, 0).astype(jnp.bfloat16)

    lay_keys(pick, source, keys, REC_BLOCKS)

    absorb_blocks(REC_BLOCKS, rec_first, rec_valid, query_rows, keys, peak, total, acc, even, odd)
    for t in range(0, 32, 8):
        parts = []
        for r in range(4):
            part = acc[r, t * 8 : t * 8 + 64] * (1.0 / total[r, t * 8 : t * 8 + 64, :1])
            parts.append(part.reshape(8, 8, LAT))
        out[t : t + 8] = jnp.concatenate(parts, 1).astype(jnp.bfloat16)


def attend_received(route, plan, boxes, own, state):
    smem, vmem = pl.BlockSpec(memory_space=pltpu.SMEM), pl.BlockSpec(memory_space=pltpu.VMEM)
    return pl.pallas_call(
        received_kernel,
        out_shape=jax.ShapeDtypeStruct((32, 32, LAT), jnp.bfloat16),
        in_specs=[smem] * 4 + [vmem] * 8,
        out_specs=vmem,
        scratch_shapes=[
            pltpu.VMEM((REC_BLOCKS, KEYS, KVW), jnp.bfloat16),
            pltpu.VMEM((ROWS, KEYS), jnp.float32),
            pltpu.VMEM((ROWS, KEYS), jnp.float32),
            pltpu.VMEM((4, ROWS, 128), jnp.float32),
            pltpu.VMEM((4, ROWS, 128), jnp.float32),
            pltpu.VMEM((4, ROWS, LAT), jnp.float32),
        ],
        compiler_params=pltpu.CompilerParams(vmem_limit_bytes=20 * MIB),
        name="attend_received",
    )(route, *plan, *boxes, own, *state)


def product(rows, weight, store):
    width = PRODUCT_WIDTH

    def part(n, _):
        lanes = pl.ds(pl.multiple_of(n * width, 128), width)
        store(lanes, jnp.dot(rows, weight[:, lanes], preferred_element_type=jnp.float32))
        return 0

    lax.fori_loop(0, weight.shape[1] // width, part, 0, unroll=True)


def store_blocks(outs):
    def store(lanes, got):
        for k, out in enumerate(outs):
            out[:, lanes] = got[k * 32 : k * 32 + 32].astype(jnp.bfloat16)

    return store


def values_kernel(order, rows, value_up, out_proj, values_out, *theirs):
    wide = jnp.concatenate([value_up[h] for h in range(4)], 1)
    all_heads = jnp.dot(rows[...], wide, preferred_element_type=jnp.float32)
    at, column = iota((1024, 512), 0), iota((1024, 512), 1)
    own_head = ((at >> 1) & 3) == (column >> 7)
    values = jnp.where(own_head, all_heads, 0.0).astype(jnp.bfloat16)
    n = iota((256, 1024), 1)
    token = (n >> 5) * 8 + ((n >> 3) & 3) * 2 + (n & 1)
    pick = (order[...] == token).astype(jnp.float32).astype(jnp.bfloat16)
    values = jnp.dot(pick, values, preferred_element_type=jnp.float32).astype(jnp.bfloat16)
    values_out[...] = values[:128]
    product(values[128:], out_proj, store_blocks(theirs))


def project_values(order, rows, value_up, out_proj):
    vmem = pl.BlockSpec(memory_space=pltpu.VMEM)
    width = out_proj.shape[1]
    return pl.pallas_call(
        values_kernel,
        out_shape=[jax.ShapeDtypeStruct((128, 512), jnp.bfloat16)]
        + [jax.ShapeDtypeStruct((32, width), jnp.bfloat16)] * 4,
        in_specs=[vmem] * 4,
        out_specs=[vmem] * 5,
        compiler_params=pltpu.CompilerParams(vmem_limit_bytes=20 * MIB),
        cost_estimate=pl.CostEstimate(flops=2_500_000_000, bytes_accessed=12_000_000, transcendentals=0),
        name="values",
    )(order, rows, value_up, out_proj)


def project_kernel(rows, weight, *outs):
    def store(lanes, got):
        for k, out in enumerate(outs):
            out[:, lanes] = got[k * 32 : k * 32 + 32]

    product(rows[...], weight, store)


def project(rows, weight):
    vmem = pl.BlockSpec(memory_space=pltpu.VMEM)
    width = weight.shape[1]
    return pl.pallas_call(
        project_kernel,
        out_shape=[jax.ShapeDtypeStruct((32, width), jnp.float32)] * 4,
        in_specs=[vmem] * 2,
        out_specs=[vmem] * 4,
        compiler_params=pltpu.CompilerParams(vmem_limit_bytes=16 * MIB),
        cost_estimate=pl.CostEstimate(flops=1_000_000_000, bytes_accessed=11_000_000, transcendentals=0),
        name="project",
    )(rows, weight)


def hidden_kernel(*refs):
    rows, (gate_weight, up_weight, down_weight, act_out), theirs = refs[:8], refs[8:12], refs[12:16]
    gate, up_part = refs[16:]
    width = HIDDEN_WIDTH
    for n in range(rows[0].shape[1] // width):
        lanes = slice(n * width, n * width + width)
        block = jnp.concatenate([row[:, lanes] for row in rows], 0)
        for total, weight in ((gate, gate_weight), (up_part, up_weight)):
            got = lax.dot_general(weight[:, lanes], block, NT, preferred_element_type=jnp.float32)
            total[...] = got if n == 0 else total[...] + got
    g = gate[...]
    act = (g / (1.0 + jnp.exp(-g)) * up_part[...]).T.astype(jnp.bfloat16)
    act_out[...] = act[:128]
    product(act[128:], down_weight, store_blocks(theirs))


def hidden_units(rows, gate_weight, up_weight, down_weight):
    vmem = pl.BlockSpec(memory_space=pltpu.VMEM)
    units, width = down_weight.shape
    return pl.pallas_call(
        hidden_kernel,
        out_shape=[jax.ShapeDtypeStruct((128, units), jnp.bfloat16)]
        + [jax.ShapeDtypeStruct((32, width), jnp.bfloat16)] * 4,
        in_specs=[vmem] * 11,
        out_specs=[vmem] * 5,
        scratch_shapes=[pltpu.VMEM((units, 256), jnp.float32)] * 2,
        compiler_params=pltpu.CompilerParams(vmem_limit_bytes=20 * MIB),
        cost_estimate=pl.CostEstimate(flops=3_000_000_000, bytes_accessed=18_000_000, transcendentals=80_000),
        name="hidden_units",
    )(*rows, gate_weight.T, up_weight.T, down_weight)


def shards(
    residual,
    queries,
    fresh_latents,
    cache_pages,
    prefill_pages,
    prefill_owner,
    prefill_slot,
    page_lists,
    context_len,
    value_up,
    out_proj,
    norm_gain,
    gate_weight,
    up_weight,
    down_weight,
):
    route = ((prefill_owner - lax.axis_index("grp")) & 3) * 16 + prefill_slot
    boxes = outbox(route, prefill_pages)
    boxes = [
        lax.ppermute(box, "grp", [(g, (g + k) % 4) for g in range(4)])
        for k, box in enumerate(boxes, 1)
    ]
    *state, slot_row, rec_valid, rec_first, out_proj = attend_resident(
        page_lists, context_len, queries, fresh_latents, cache_pages, out_proj
    )
    attended = attend_received(
        route, (slot_row, rec_valid, rec_first), boxes, prefill_pages, state
    )
    by_heads = lax.all_to_all(attended, "tp", split_axis=0, concat_axis=0, tiled=True)
    values, *theirs = project_values(token_order()[:, None], by_heads.reshape(1024, LAT), value_up, out_proj)
    terms = reduce_first(project(values, out_proj), theirs)
    hidden, normed = settle(terms, residual, norm_gain)
    act, *theirs = hidden_units(gather_first(normed), gate_weight, up_weight, down_weight)
    mlp = reduce_second(reduce_first(project(act, down_weight), theirs))
    return (hidden.astype(jnp.float32) + mlp).astype(jnp.bfloat16)


def solution(mesh):
    placed = (
        P(("grp", "tp"), None),
        P(("grp", "tp"), None),
        P(("grp", "tp"), None),
        P(("grp", "tp"), None),
        P(("grp", "tp"), None),
        P(("grp", "tp")),
        P(("grp", "tp")),
        P(("grp", "tp"), None),
        P(("grp", "tp")),
        P("tp", None, None),
        P("tp", None),
        P(),
        P(None, "tp"),
        P(None, "tp"),
        P("tp", None),
    )
    return jax.shard_map(
        shards, mesh=mesh, in_specs=placed, out_specs=P(("grp", "tp"), None), check_vma=False
    )
```

```python
import math

import jax
import jax.numpy as jnp
from jax import lax
from jax.experimental import pallas as pl
from jax.experimental.pallas import tpu as pltpu
from jax.sharding import PartitionSpec as P

HEADS = 128
LAT = 512
ROPE = 64
HEADV = 128
PAGE = 64
KVW = 576
MOST = 8
PAGE_WIDTH = PAGE * KVW
PAIR = 2 * KVW
RES_BLOCKS = 11
UNROLL = 16
CUTS = (1792, 5376)
PRODUCT_WIDTH = 256
HIDDEN_WIDTH = 1792
REC_BLOCKS = 5
RES_SPARE = (RES_BLOCKS + 1) * 8
REC_SPARE = (REC_BLOCKS + 1) * 8
KEYS = 8 * PAGE
LOW = -1e30
EXPONENT = (HEADV + ROPE) ** (-0.5) * math.log2(math.e)
ROWS = 2 * HEADS
NT = (((1,), (1,)), ((), ()))
MIB = 1024 * 1024


def chip_pairs(step0, step1):
    pairs = []
    for y in range(4):
        for x in range(4):
            for core, (dy, dx, flip) in enumerate((step0, step1)):
                there = (((y + dy) % 4) * 4 + (x + dx) % 4) * 2 + (core ^ flip)
                pairs.append(((y * 4 + x) * 2 + core, there))
    return pairs


def swap_cores(block):
    return lax.ppermute(block, "tp", chip_pairs((0, 0, 1), (0, 0, 1)))


def along_first(block, k):
    return lax.ppermute(block, "tp", chip_pairs((0, k, 0), (k, 0, 0)))


def along_second(block, k):
    return lax.ppermute(block, "tp", chip_pairs((k, 0, 0), (0, k, 0)))


def token_order():
    t = lax.axis_index("tp")
    y, x, core = t // 8, (t // 2) % 4, t % 2
    row = jnp.arange(256, dtype=jnp.int32)
    owner_core = jnp.where(row // 128 == 0, core, 1 - core)
    k1, k2, i = (row // 32) % 4, (row // 8) % 4, row % 8
    dy = jnp.where(owner_core == 0, k2, k1)
    dx = jnp.where(owner_core == 0, k1, k2)
    return ((((y + dy) % 4) * 4 + (x + dx) % 4) * 2 + owner_core) * 8 + i


def add_up(own, others):
    total = own.astype(jnp.float32)
    for other in others:
        total = total + other.astype(jnp.float32)
    return total


def reduce_first(mine, theirs):
    got = {k: swap_cores(theirs[k]) for k in (1, 3, 2, 0)}
    chunks = {k: add_up(mine[k], [got[k]]).astype(jnp.bfloat16) for k in (1, 3, 2)}
    return [mine[0], got[0]] + [along_first(chunks[k], k) for k in (1, 3, 2)]


def reduce_second(terms):
    chunks = add_up(terms[0], terms[1:]).reshape(4, 8, -1)
    arrived = [along_second(chunks[k].astype(jnp.bfloat16), k) for k in (1, 3, 2)]
    return add_up(chunks[0], arrived)


def share_kernel(residual, *refs):
    terms, (total, sent) = refs[:-2], refs[-2:]
    for n in range(0, total.shape[1], 1024):
        lanes = slice(n, n + 1024)
        own = terms[0][:, lanes]
        for term in terms[1:]:
            own = own + term[:, lanes].astype(jnp.float32)
        first = own[:8] + residual[:, lanes].astype(jnp.float32)
        own = jnp.concatenate([first, own[8:]], 0)
        total[:, lanes] = own
        sent[:, lanes] = own.astype(jnp.bfloat16)


def settle_kernel(total, got1, got2, got3, norm_gain, hidden_out, normed, hidden):
    width = total.shape[1]
    squares = jnp.zeros((32, 1), jnp.float32)
    for n in range(0, width, 1024):
        lanes = slice(n, n + 1024)
        block = total[:, lanes]
        for k, got in ((1, got1), (2, got2), (3, got3)):
            got = got[:, lanes].astype(jnp.float32)
            block = block + jnp.concatenate([got[k * 8 :], got[: k * 8]], 0)
        block = block.astype(jnp.bfloat16)
        hidden_out[:, lanes] = block[:8]
        block = block.astype(jnp.float32)
        hidden[:, lanes] = block
        squares = squares + jnp.sum(block * block, -1, keepdims=True)
    spread = lax.rsqrt(squares * (1.0 / width) + 1e-06)
    for n in range(0, width, 1024):
        lanes = slice(n, n + 1024)
        gain = norm_gain[:, lanes].astype(jnp.float32)
        normed[:, lanes] = (hidden[:, lanes] * spread * gain).astype(jnp.bfloat16)


def settle(terms, residual, norm_gain):
    vmem = pl.BlockSpec(memory_space=pltpu.VMEM)
    params = pltpu.CompilerParams(vmem_limit_bytes=12 * MIB)
    shape = terms[0].shape
    total, sent = pl.pallas_call(
        share_kernel,
        out_shape=[jax.ShapeDtypeStruct(shape, jnp.float32), jax.ShapeDtypeStruct(shape, jnp.bfloat16)],
        in_specs=[vmem] * 6,
        out_specs=[vmem] * 2,
        compiler_params=params,
        name="share",
    )(residual, *terms)
    got = {k: along_second(sent, k) for k in (1, 3, 2)}
    return pl.pallas_call(
        settle_kernel,
        out_shape=[
            jax.ShapeDtypeStruct(residual.shape, jnp.bfloat16),
            jax.ShapeDtypeStruct(shape, jnp.bfloat16),
        ],
        in_specs=[vmem] * 5,
        out_specs=[vmem] * 2,
        scratch_shapes=[pltpu.VMEM(shape, jnp.float32)],
        compiler_params=params,
        name="settle",
    )(total, got[1], got[2], got[3], norm_gain[None, :])


def gather_first(rows):
    arrived = {k: along_first(rows, 4 - k) for k in (1, 3, 2)}
    mine = [rows] + [arrived[k] for k in (1, 2, 3)]
    return mine + [swap_cores(part) for part in mine]


def iota(shape, dim):
    return lax.broadcasted_iota(jnp.int32, shape, dim)


def outbox_kernel(route, pages, out1, out2, out3):
    outs = (out1, out2, out3)
    rows, cols = iota((32, 128), 0), iota((32, 128), 1)
    pick = jnp.zeros((32, 128), jnp.float32)
    slots = jnp.full((32, 128), 64, jnp.int32)
    counts = [jnp.int32(0)] * 4
    for i in range(16):
        step = route[i] >> 4
        rank = jnp.int32(0)
        for k in range(1, 4):
            rank = jnp.where(step == k, counts[k], rank)
            counts[k] = counts[k] + jnp.where(step == k, 1, 0)
        target = jnp.where(step == 0, -1, (step - 1) * MOST + rank)
        pick = jnp.where((rows == target) & (cols == i), 1.0, pick)
        slots = jnp.where(rows == target, route[i] & 15, slots)
    pick = pick[:, :16].astype(jnp.bfloat16)
    slots = slots.astype(jnp.float32).astype(jnp.bfloat16)

    def chunk(n, _):
        for u in range(UNROLL):
            lanes = pl.ds(pl.multiple_of((n * UNROLL + u) * PAIR, 128), PAIR)
            got = jnp.dot(pick, pages[:, lanes], preferred_element_type=jnp.float32)
            for k in range(3):
                outs[k][:, lanes] = got[k * 8 : k * 8 + 8].astype(jnp.bfloat16)
        return 0

    lax.fori_loop(0, PAGE // 2 // UNROLL, chunk, 0)
    for k in range(3):
        outs[k][:, PAGE_WIDTH:] = slots[k * 8 : k * 8 + 8]


def outbox(route, pages):
    smem, vmem = pl.BlockSpec(memory_space=pltpu.SMEM), pl.BlockSpec(memory_space=pltpu.VMEM)
    return pl.pallas_call(
        outbox_kernel,
        out_shape=[jax.ShapeDtypeStruct((MOST, PAGE_WIDTH + 128), jnp.bfloat16)] * 3,
        in_specs=[smem, vmem],
        out_specs=[vmem] * 3,
        compiler_params=pltpu.CompilerParams(vmem_limit_bytes=16 * MIB),
        name="outbox",
    )(route, pages)


def lay_keys(pick, source, keys, blocks):
    def chunk(n, _):
        for u in range(UNROLL):
            at = n * UNROLL + u
            lanes = pl.ds(pl.multiple_of(at * PAIR, 128), PAIR)
            got = jnp.dot(pick, source(lanes), preferred_element_type=jnp.float32)
            even = got[: blocks * 8, :KVW].reshape(blocks, 8, KVW)
            odd = got[: blocks * 8, KVW:].reshape(blocks, 8, KVW)
            both = jnp.concatenate([even, odd], 1).astype(jnp.bfloat16)
            keys[:, pl.ds(pl.multiple_of(at * 16, 16), 16), :] = both
        return 0

    lax.fori_loop(0, PAGE // 2 // UNROLL, chunk, 0)


def key_limit(first, valid):
    at = iota((8, KEYS), 1)
    limit = jnp.zeros((8, KEYS), jnp.int32)
    for i in range(8):
        limit = jnp.where((at & 7) == i, valid[first + i], limit)
    return ((at >> 3) < limit)[:1]


def absorb(scores, live, value_rows, peak, total, acc, r):
    scores = jnp.where(live, scores * EXPONENT, LOW)
    before = peak[r]
    top = jnp.maximum(before, jnp.max(scores, -1, keepdims=True))
    weight = jnp.exp2(scores - top[:, :1])
    fade = jnp.exp2(before - top)
    peak[r] = top
    total[r] = total[r] * fade + jnp.sum(weight, -1, keepdims=True)
    acc[r] = acc[r] * fade[:, :1] + jnp.dot(
        weight.astype(jnp.bfloat16), value_rows, preferred_element_type=jnp.float32
    )


def absorb_blocks(blocks, first, valid, query_rows, keys, peak, total, acc, even, odd):
    def request_of(b):
        r = jnp.int32(0)
        for n in range(1, 4):
            r = r + jnp.where(b >= first[n], 1, 0)
        return r

    def scores_of(b):
        return lax.dot_general(
            query_rows[request_of(b)], keys[jnp.minimum(b, blocks - 1)], NT, preferred_element_type=jnp.float32
        )

    def take(b, scores):
        value_rows = keys[jnp.minimum(b, blocks - 1), :, :LAT]
        absorb(scores[...], key_limit(b * 8, valid), value_rows, peak, total, acc, request_of(b))

    even[...] = scores_of(0)

    def step(n, _):
        odd[...] = scores_of(2 * n + 1)
        take(2 * n, even)
        even[...] = scores_of(2 * n + 2)
        take(2 * n + 1, odd)
        return 0

    lax.fori_loop(0, (first[4] + 1) // 2, step, 0)


def resident_kernel(
    lists, lengths, queries, fresh, cache,
    query_rows, peak, total, acc, slot_row, rec_valid, rec_first,
    keys, even, odd, head_rows, res_page, res_valid, res_first,
):
    for i in range(RES_BLOCKS * 8):
        res_page[i] = 0
    for i in range(RES_SPARE):
        res_valid[i] = 0
    for i in range(REC_SPARE):
        rec_valid[i] = 0
    for i in range(17):
        slot_row[i] = 0
    res_at, rec_at = jnp.int32(0), jnp.int32(0)
    for r in range(4):
        res_first[r] = res_at // 8
        rec_first[r] = rec_at // 8
        length = lengths[r]

        def page(p, carry):
            res_at, rec_at = carry
            entry = lists[r, p]
            live = jnp.minimum(length - p * PAGE, PAGE)
            resident = entry < 64
            at = jnp.where(resident, res_at, RES_SPARE)
            res_page[at] = entry
            res_valid[at] = live
            at = jnp.where(resident, REC_SPARE, rec_at)
            rec_valid[at] = live
            slot_row[jnp.where(resident, 16, entry - 64)] = rec_at
            one = jnp.where(resident, 1, 0)
            return res_at + one, rec_at + 1 - one

        res_at, rec_at = lax.fori_loop(0, (length + PAGE - 1) // PAGE, page, (res_at, rec_at))
        res_at = (res_at + 7) // 8 * 8
        rec_at = (rec_at + 7) // 8 * 8
    res_first[4] = res_at // 8
    rec_first[4] = rec_at // 8

    to, of = iota((128, 128), 0), iota((128, 128), 1)
    wanted = ((to >> 1) & 15) * 8 + (to >> 5) * 2 + (to & 1)
    order = (wanted == of).astype(jnp.float32).astype(jnp.bfloat16)
    for g in range(HEADS // 16):
        for n in range(8):
            two = queries[:, (g * 8 + n) * PAIR : (g * 8 + n + 1) * PAIR].astype(jnp.float32)
            head_rows[pl.ds(n * 16, 16), :] = jnp.concatenate(
                [two[:, :KVW], two[:, KVW:]], 0
            ).astype(jnp.bfloat16)
        placed = jnp.dot(order, head_rows[...], preferred_element_type=jnp.float32).astype(jnp.bfloat16)
        for r in range(4):
            query_rows[r, g * 32 : g * 32 + 32, :] = placed[r * 32 : r * 32 + 32]

    new_keys = jnp.concatenate([fresh[...].astype(jnp.float32), jnp.zeros((120, KVW), jnp.float32)], 0).astype(jnp.bfloat16)
    for r in range(4):
        scores = lax.dot_general(query_rows[r], new_keys, NT, preferred_element_type=jnp.float32) * EXPONENT
        column, j = iota((ROWS, 128), 1), iota((ROWS, 128), 0) & 1
        seen = (column == 2 * r) | ((column == 2 * r + 1) & (j == 1))
        scores = jnp.where(seen, scores, LOW)
        top = jnp.max(scores, -1, keepdims=True)
        weight = jnp.exp2(scores - top)
        peak[r] = jnp.broadcast_to(top, (ROWS, 128))
        total[r] = jnp.broadcast_to(jnp.sum(weight, -1, keepdims=True), (ROWS, 128))
        acc[r] = jnp.dot(weight.astype(jnp.bfloat16), new_keys[:, :LAT], preferred_element_type=jnp.float32)

    pick = []
    sub, lane = iota((8, 64), 0), iota((8, 64), 1)
    for b in range(RES_BLOCKS):
        source = jnp.zeros((8, 64), jnp.int32)
        for i in range(8):
            source = jnp.where(sub == i, res_page[b * 8 + i], source)
        pick.append((source == lane).astype(jnp.float32))
    pick.append(jnp.zeros((8, 64), jnp.float32))
    pick = jnp.concatenate(pick, 0).astype(jnp.bfloat16)
    lay_keys(pick, lambda lanes: cache[:, lanes], keys, RES_BLOCKS)

    absorb_blocks(RES_BLOCKS, res_first, res_valid, query_rows, keys, peak, total, acc, even, odd)


def attend_resident(lists, lengths, queries, fresh, cache):
    smem, vmem = pl.BlockSpec(memory_space=pltpu.SMEM), pl.BlockSpec(memory_space=pltpu.VMEM)
    shapes = [
        jax.ShapeDtypeStruct((4, ROWS, KVW), jnp.bfloat16),
        jax.ShapeDtypeStruct((4, ROWS, 128), jnp.float32),
        jax.ShapeDtypeStruct((4, ROWS, 128), jnp.float32),
        jax.ShapeDtypeStruct((4, ROWS, LAT), jnp.float32),
        jax.ShapeDtypeStruct((24,), jnp.int32),
        jax.ShapeDtypeStruct((REC_SPARE + 8,), jnp.int32),
        jax.ShapeDtypeStruct((8,), jnp.int32),
    ]
    return pl.pallas_call(
        resident_kernel,
        out_shape=shapes,
        in_specs=[smem, smem, vmem, vmem, vmem],
        out_specs=[vmem] * 4 + [smem] * 3,
        scratch_shapes=[
            pltpu.VMEM((RES_BLOCKS, KEYS, KVW), jnp.bfloat16),
            pltpu.VMEM((ROWS, KEYS), jnp.float32),
            pltpu.VMEM((ROWS, KEYS), jnp.float32),
            pltpu.VMEM((128, KVW), jnp.bfloat16),
            pltpu.SMEM((RES_SPARE + 8,), jnp.int32),
            pltpu.SMEM((RES_SPARE + 8,), jnp.int32),
            pltpu.SMEM((8,), jnp.int32),
        ],
        compiler_params=pltpu.CompilerParams(vmem_limit_bytes=20 * MIB),
        cost_estimate=pl.CostEstimate(flops=8_000_000_000, bytes_accessed=12_000_000, transcendentals=2_000_000),
        name="attend_resident",
    )(lists, lengths, queries, fresh, cache)


def received_kernel(
    route, slot_row, rec_valid, rec_first,
    box1, box2, box3, own, query_rows, peak_in, total_in, acc_in,
    out, keys, even, odd, peak, total, acc, sems,
):
    state = [
        pltpu.make_async_copy(kept, held, sems.at[n])
        for n, (kept, held) in enumerate(((peak_in, peak), (total_in, total), (acc_in, acc)))
    ]
    for copy in state:
        copy.start()
    boxes = (box1, box2, box3)
    cols = iota((24, 128), 1)
    slots = jnp.concatenate([box[:, PAGE_WIDTH:].astype(jnp.float32) for box in boxes], 0)
    arrived = jnp.zeros((24, 128), jnp.float32)
    for n in range(16):
        arrived = jnp.where((slots == float(n)) & (cols == slot_row[n]), 1.0, arrived)
    rows, cols = iota((16, 128), 0), iota((16, 128), 1)
    kept = jnp.zeros((16, 128), jnp.float32)
    for i in range(16):
        target = jnp.where(route[i] >> 4 == 0, slot_row[route[i] & 15], -1)
        kept = jnp.where((rows == i) & (cols == target), 1.0, kept)
    place_of = jnp.concatenate([arrived, kept, jnp.zeros((88, 128), jnp.float32)], 0)
    pick = place_of.T[:48, :48].astype(jnp.bfloat16)

    def source(lanes):
        parts = [box[:, lanes].astype(jnp.float32) for box in boxes]
        parts.append(own[:, lanes].astype(jnp.float32))
        parts.append(jnp.zeros((8, PAIR), jnp.float32))
        return jnp.concatenate(parts, 0).astype(jnp.bfloat16)

    lay_keys(pick, source, keys, REC_BLOCKS)
    for copy in state:
        copy.wait()
    absorb_blocks(REC_BLOCKS, rec_first, rec_valid, query_rows, keys, peak, total, acc, even, odd)
    for t in range(0, 32, 8):
        parts = []
        for r in range(4):
            part = acc[r, t * 8 : t * 8 + 64] * (1.0 / total[r, t * 8 : t * 8 + 64, :1])
            parts.append(part.reshape(8, 8, LAT))
        out[t : t + 8] = jnp.concatenate(parts, 1).astype(jnp.bfloat16)


def attend_received(route, plan, boxes, own, state):
    smem, vmem = pl.BlockSpec(memory_space=pltpu.SMEM), pl.BlockSpec(memory_space=pltpu.VMEM)
    return pl.pallas_call(
        received_kernel,
        out_shape=jax.ShapeDtypeStruct((32, 32, LAT), jnp.bfloat16),
        in_specs=[smem] * 4 + [vmem] * 8,
        out_specs=vmem,
        scratch_shapes=[
            pltpu.VMEM((REC_BLOCKS, KEYS, KVW), jnp.bfloat16),
            pltpu.VMEM((ROWS, KEYS), jnp.float32),
            pltpu.VMEM((ROWS, KEYS), jnp.float32),
            pltpu.VMEM((4, ROWS, 128), jnp.float32),
            pltpu.VMEM((4, ROWS, 128), jnp.float32),
            pltpu.VMEM((4, ROWS, LAT), jnp.float32),
            pltpu.SemaphoreType.DMA((3,)),
        ],
        compiler_params=pltpu.CompilerParams(vmem_limit_bytes=20 * MIB),
        name="attend_received",
    )(route, *plan, *boxes, own, *state)


def product(rows, weights, store):
    start = 0
    for weight in weights:
        for at in range(0, weight.shape[1], PRODUCT_WIDTH):
            got = jnp.dot(rows, weight[:, at : at + PRODUCT_WIDTH], preferred_element_type=jnp.float32)
            store(slice(start + at, start + at + PRODUCT_WIDTH), got)
        start += weight.shape[1]


def store_blocks(outs):
    def store(lanes, got):
        for k, out in enumerate(outs):
            out[:, lanes] = got[k * 32 : k * 32 + 32].astype(out.dtype)

    return store


def stage_kernel(_after, weight, *refs):
    staged, sems = refs[:-1], refs[-1]
    copies, start = [], 0
    for n, out in enumerate(staged):
        width = out.shape[1]
        copies.append(pltpu.make_async_copy(weight.at[:, pl.ds(start, width)], out, sems.at[n]))
        copies[n].start()
        start += width
    for copy in copies:
        copy.wait()


def stage(after, weight):
    anywhere = pl.BlockSpec(memory_space=pl.ANY)
    return pl.pallas_call(
        stage_kernel,
        out_shape=[jax.ShapeDtypeStruct((weight.shape[0], width), weight.dtype) for width in CUTS],
        in_specs=[anywhere] * 2,
        out_specs=[pl.BlockSpec(memory_space=pltpu.VMEM)] * len(CUTS),
        scratch_shapes=[pltpu.SemaphoreType.DMA((len(CUTS),))],
        compiler_params=pltpu.CompilerParams(vmem_limit_bytes=4 * MIB),
        cost_estimate=pl.CostEstimate(flops=4_000_000_000, bytes_accessed=15_000_000, transcendentals=0),
        name="stage",
    )(after, weight)


def values_kernel(order, rows, value_up, mine, theirs):
    wide = jnp.concatenate([value_up[h] for h in range(4)], 1)
    all_heads = jnp.dot(rows[...], wide, preferred_element_type=jnp.float32)
    at, column = iota((1024, 512), 0), iota((1024, 512), 1)
    own_head = ((at >> 1) & 3) == (column >> 7)
    values = jnp.where(own_head, all_heads, 0.0).astype(jnp.bfloat16)
    n = iota((256, 1024), 1)
    token = (n >> 5) * 8 + ((n >> 3) & 3) * 2 + (n & 1)
    pick = (order[...] == token).astype(jnp.float32).astype(jnp.bfloat16)
    values = jnp.dot(pick, values, preferred_element_type=jnp.float32).astype(jnp.bfloat16)
    mine[...] = values[:128]
    theirs[...] = values[128:]


def find_values(order, rows, value_up):
    vmem = pl.BlockSpec(memory_space=pltpu.VMEM)
    return pl.pallas_call(
        values_kernel,
        out_shape=[jax.ShapeDtypeStruct((128, 512), jnp.bfloat16)] * 2,
        in_specs=[vmem] * 3,
        out_specs=[vmem] * 2,
        compiler_params=pltpu.CompilerParams(vmem_limit_bytes=16 * MIB),
        cost_estimate=pl.CostEstimate(flops=4_000_000_000, bytes_accessed=4_000_000, transcendentals=0),
        name="values",
    )(order, rows, value_up)


def project_kernel(rows, *refs):
    product(rows[...], refs[:-4], store_blocks(refs[-4:]))


def project(rows, weights, dtype):
    vmem = pl.BlockSpec(memory_space=pltpu.VMEM)
    width = sum(weight.shape[1] for weight in weights)
    return pl.pallas_call(
        project_kernel,
        out_shape=[jax.ShapeDtypeStruct((32, width), dtype)] * 4,
        in_specs=[vmem] * (1 + len(weights)),
        out_specs=[vmem] * 4,
        compiler_params=pltpu.CompilerParams(vmem_limit_bytes=16 * MIB),
        cost_estimate=pl.CostEstimate(flops=1_000_000_000, bytes_accessed=11_000_000, transcendentals=0),
        name="project",
    )(rows, *weights)


def hidden_kernel(*refs):
    rows, (gate_weight, up_weight, down_weight, act_out), theirs = refs[:8], refs[8:12], refs[12:16]
    gate, up_part = refs[16:]
    width = HIDDEN_WIDTH
    for n in range(rows[0].shape[1] // width):
        lanes = slice(n * width, n * width + width)
        block = jnp.concatenate([row[:, lanes] for row in rows], 0)
        for total, weight in ((gate, gate_weight), (up_part, up_weight)):
            got = lax.dot_general(weight[:, lanes], block, NT, preferred_element_type=jnp.float32)
            total[...] = got if n == 0 else total[...] + got
    g = gate[...]
    act = (g / (1.0 + jnp.exp(-g)) * up_part[...]).T.astype(jnp.bfloat16)
    act_out[...] = act[:128]
    product(act[128:], [down_weight], store_blocks(theirs))


def hidden_units(rows, gate_weight, up_weight, down_weight):
    vmem = pl.BlockSpec(memory_space=pltpu.VMEM)
    units, width = down_weight.shape
    return pl.pallas_call(
        hidden_kernel,
        out_shape=[jax.ShapeDtypeStruct((128, units), jnp.bfloat16)]
        + [jax.ShapeDtypeStruct((32, width), jnp.bfloat16)] * 4,
        in_specs=[vmem] * 11,
        out_specs=[vmem] * 5,
        scratch_shapes=[pltpu.VMEM((units, 256), jnp.float32)] * 2,
        compiler_params=pltpu.CompilerParams(vmem_limit_bytes=20 * MIB),
        cost_estimate=pl.CostEstimate(flops=3_000_000_000, bytes_accessed=18_000_000, transcendentals=80_000),
        name="hidden_units",
    )(*rows, gate_weight.T, up_weight.T, down_weight)


def shards(
    residual,
    queries,
    fresh_latents,
    cache_pages,
    prefill_pages,
    prefill_owner,
    prefill_slot,
    page_lists,
    context_len,
    value_up,
    out_proj,
    norm_gain,
    gate_weight,
    up_weight,
    down_weight,
):
    route = ((prefill_owner - lax.axis_index("grp")) & 3) * 16 + prefill_slot
    boxes = outbox(route, prefill_pages)
    boxes = {k: lax.ppermute(boxes[k - 1], "grp", [(g, (g + k) % 4) for g in range(4)]) for k in (1, 3, 2)}
    boxes = [boxes[k] for k in (1, 2, 3)]
    *state, slot_row, rec_valid, rec_first = attend_resident(
        page_lists, context_len, queries, fresh_latents, cache_pages
    )
    attended = attend_received(
        route, (slot_row, rec_valid, rec_first), boxes, prefill_pages, state
    )
    out_proj = stage(attended, out_proj)
    by_heads = lax.all_to_all(attended, "tp", split_axis=0, concat_axis=0, tiled=True)
    mine, theirs = find_values(token_order()[:, None], by_heads.reshape(1024, LAT), value_up)
    theirs = project(theirs, out_proj, jnp.bfloat16)
    terms = reduce_first(project(mine, out_proj, jnp.float32), theirs)
    hidden, normed = settle(terms, residual, norm_gain)
    act, *theirs = hidden_units(gather_first(normed), gate_weight, up_weight, down_weight)
    mlp = reduce_second(reduce_first(project(act, [down_weight], jnp.float32), theirs))
    return (hidden.astype(jnp.float32) + mlp).astype(jnp.bfloat16)


def solution(mesh):
    placed = (
        P(("grp", "tp"), None),
        P(("grp", "tp"), None),
        P(("grp", "tp"), None),
        P(("grp", "tp"), None),
        P(("grp", "tp"), None),
        P(("grp", "tp")),
        P(("grp", "tp")),
        P(("grp", "tp"), None),
        P(("grp", "tp")),
        P("tp", None, None),
        P("tp", None),
        P(),
        P(None, "tp"),
        P(None, "tp"),
        P("tp", None),
    )
    return jax.shard_map(
        shards, mesh=mesh, in_specs=placed, out_specs=P(("grp", "tp"), None), check_vma=False
    )
```

```python
import math

import jax
import jax.numpy as jnp
from jax import lax
from jax.experimental import pallas as pl
from jax.experimental.pallas import tpu as pltpu
from jax.sharding import PartitionSpec as P

HEADS = 128
LAT = 512
ROPE = 64
HEADV = 128
PAGE = 64
KVW = 576
MOST = 8
PAGE_WIDTH = PAGE * KVW
PAIR = 2 * KVW
RES_BLOCKS = 11
UNROLL = 16
CUTS = (1792, 5376)
PRODUCT_WIDTH = 256
HIDDEN_WIDTH = 1792
REC_BLOCKS = 5
RES_SPARE = (RES_BLOCKS + 1) * 8
REC_SPARE = (REC_BLOCKS + 1) * 8
KEYS = 8 * PAGE
LOW = -1e30
EXPONENT = (HEADV + ROPE) ** (-0.5) * math.log2(math.e)
ROWS = 2 * HEADS
NT = (((1,), (1,)), ((), ()))
MIB = 1024 * 1024


def chip_pairs(step0, step1):
    pairs = []
    for y in range(4):
        for x in range(4):
            for core, (dy, dx, flip) in enumerate((step0, step1)):
                there = (((y + dy) % 4) * 4 + (x + dx) % 4) * 2 + (core ^ flip)
                pairs.append(((y * 4 + x) * 2 + core, there))
    return pairs


def swap_cores(block):
    return lax.ppermute(block, "tp", chip_pairs((0, 0, 1), (0, 0, 1)))


def along_first(block, k):
    return lax.ppermute(block, "tp", chip_pairs((0, k, 0), (k, 0, 0)))


def along_second(block, k):
    return lax.ppermute(block, "tp", chip_pairs((k, 0, 0), (0, k, 0)))


def token_order():
    t = lax.axis_index("tp")
    y, x, core = t // 8, (t // 2) % 4, t % 2
    row = jnp.arange(256, dtype=jnp.int32)
    owner_core = jnp.where(row // 128 == 0, core, 1 - core)
    k1, k2, i = (row // 32) % 4, (row // 8) % 4, row % 8
    dy = jnp.where(owner_core == 0, k2, k1)
    dx = jnp.where(owner_core == 0, k1, k2)
    return ((((y + dy) % 4) * 4 + (x + dx) % 4) * 2 + owner_core) * 8 + i


def add_up(own, others):
    total = own.astype(jnp.float32)
    for other in others:
        total = total + other.astype(jnp.float32)
    return total


def reduce_first(mine, theirs):
    got = {k: swap_cores(theirs[k]) for k in (2, 1, 3, 0)}
    chunks = {k: add_up(mine[k], [got[k]]).astype(jnp.bfloat16) for k in (2, 1, 3)}
    return [mine[0], got[0]] + [along_first(chunks[k], k) for k in (2, 1, 3)]


def reduce_second(terms):
    chunks = add_up(terms[0], terms[1:]).reshape(4, 8, -1)
    arrived = [along_second(chunks[k].astype(jnp.bfloat16), k) for k in (1, 3, 2)]
    return add_up(chunks[0], arrived)


def share_kernel(residual, *refs):
    terms, (total, sent) = refs[:-2], refs[-2:]
    for n in range(0, total.shape[1], 1024):
        lanes = slice(n, n + 1024)
        own = terms[0][:, lanes]
        for term in terms[1:]:
            own = own + term[:, lanes].astype(jnp.float32)
        first = own[:8] + residual[:, lanes].astype(jnp.float32)
        own = jnp.concatenate([first, own[8:]], 0)
        total[:, lanes] = own
        sent[:, lanes] = own.astype(jnp.bfloat16)


def settle_kernel(total, got1, got2, got3, norm_gain, hidden_out, normed, hidden):
    width = total.shape[1]
    squares = jnp.zeros((32, 1), jnp.float32)
    for n in range(0, width, 1024):
        lanes = slice(n, n + 1024)
        block = total[:, lanes]
        for k, got in ((1, got1), (2, got2), (3, got3)):
            got = got[:, lanes].astype(jnp.float32)
            block = block + jnp.concatenate([got[k * 8 :], got[: k * 8]], 0)
        block = block.astype(jnp.bfloat16)
        hidden_out[:, lanes] = block[:8]
        block = block.astype(jnp.float32)
        hidden[:, lanes] = block
        squares = squares + jnp.sum(block * block, -1, keepdims=True)
    spread = lax.rsqrt(squares * (1.0 / width) + 1e-06)
    for n in range(0, width, 1024):
        lanes = slice(n, n + 1024)
        gain = norm_gain[:, lanes].astype(jnp.float32)
        normed[:, lanes] = (hidden[:, lanes] * spread * gain).astype(jnp.bfloat16)


def settle(terms, residual, norm_gain):
    vmem = pl.BlockSpec(memory_space=pltpu.VMEM)
    params = pltpu.CompilerParams(vmem_limit_bytes=12 * MIB)
    shape = terms[0].shape
    total, sent = pl.pallas_call(
        share_kernel,
        out_shape=[jax.ShapeDtypeStruct(shape, jnp.float32), jax.ShapeDtypeStruct(shape, jnp.bfloat16)],
        in_specs=[vmem] * 6,
        out_specs=[vmem] * 2,
        compiler_params=params,
        name="share",
    )(residual, *terms)
    got = {k: along_second(sent, k) for k in (1, 3, 2)}
    return pl.pallas_call(
        settle_kernel,
        out_shape=[
            jax.ShapeDtypeStruct(residual.shape, jnp.bfloat16),
            jax.ShapeDtypeStruct(shape, jnp.bfloat16),
        ],
        in_specs=[vmem] * 5,
        out_specs=[vmem] * 2,
        scratch_shapes=[pltpu.VMEM(shape, jnp.float32)],
        compiler_params=params,
        name="settle",
    )(total, got[1], got[2], got[3], norm_gain[None, :])


def gather_first(rows):
    arrived = {k: along_first(rows, 4 - k) for k in (2, 1, 3)}
    mine = [rows] + [arrived[k] for k in (1, 2, 3)]
    return mine + [swap_cores(part) for part in mine]


def iota(shape, dim):
    return lax.broadcasted_iota(jnp.int32, shape, dim)


def outbox_kernel(route, pages, out1, out2, out3):
    outs = (out1, out2, out3)
    rows, cols = iota((32, 128), 0), iota((32, 128), 1)
    pick = jnp.zeros((32, 128), jnp.float32)
    slots = jnp.full((32, 128), 64, jnp.int32)
    counts = [jnp.int32(0)] * 4
    for i in range(16):
        step = route[i] >> 4
        rank = jnp.int32(0)
        for k in range(1, 4):
            rank = jnp.where(step == k, counts[k], rank)
            counts[k] = counts[k] + jnp.where(step == k, 1, 0)
        target = jnp.where(step == 0, -1, (step - 1) * MOST + rank)
        pick = jnp.where((rows == target) & (cols == i), 1.0, pick)
        slots = jnp.where(rows == target, route[i] & 15, slots)
    pick = pick[:, :16].astype(jnp.bfloat16)
    slots = slots.astype(jnp.float32).astype(jnp.bfloat16)

    def chunk(n, _):
        for u in range(UNROLL):
            lanes = pl.ds(pl.multiple_of((n * UNROLL + u) * PAIR, 128), PAIR)
            got = jnp.dot(pick, pages[:, lanes], preferred_element_type=jnp.float32)
            for k in range(3):
                outs[k][:, lanes] = got[k * 8 : k * 8 + 8].astype(jnp.bfloat16)
        return 0

    lax.fori_loop(0, PAGE // 2 // UNROLL, chunk, 0)
    for k in range(3):
        outs[k][:, PAGE_WIDTH:] = slots[k * 8 : k * 8 + 8]


def outbox(route, pages):
    smem, vmem = pl.BlockSpec(memory_space=pltpu.SMEM), pl.BlockSpec(memory_space=pltpu.VMEM)
    return pl.pallas_call(
        outbox_kernel,
        out_shape=[jax.ShapeDtypeStruct((MOST, PAGE_WIDTH + 128), jnp.bfloat16)] * 3,
        in_specs=[smem, vmem],
        out_specs=[vmem] * 3,
        compiler_params=pltpu.CompilerParams(vmem_limit_bytes=16 * MIB),
        name="outbox",
    )(route, pages)


def lay_keys(pick, source, keys, blocks):
    def chunk(n, _):
        for u in range(UNROLL):
            at = n * UNROLL + u
            lanes = pl.ds(pl.multiple_of(at * PAIR, 128), PAIR)
            got = jnp.dot(pick, source(lanes), preferred_element_type=jnp.float32)
            even = got[: blocks * 8, :KVW].reshape(blocks, 8, KVW)
            odd = got[: blocks * 8, KVW:].reshape(blocks, 8, KVW)
            both = jnp.concatenate([even, odd], 1).astype(jnp.bfloat16)
            keys[:, pl.ds(pl.multiple_of(at * 16, 16), 16), :] = both
        return 0

    lax.fori_loop(0, PAGE // 2 // UNROLL, chunk, 0)


def key_limit(first, valid):
    at = iota((8, KEYS), 1)
    limit = jnp.zeros((8, KEYS), jnp.int32)
    for i in range(8):
        limit = jnp.where((at & 7) == i, valid[first + i], limit)
    return ((at >> 3) < limit)[:1]


def absorb(scores, live, value_rows, peak, total, acc, r):
    scores = jnp.where(live, scores * EXPONENT, LOW)
    before = peak[r]
    top = jnp.maximum(before, jnp.max(scores, -1, keepdims=True))
    weight = jnp.exp2(scores - top[:, :1])
    fade = jnp.exp2(before - top)
    peak[r] = top
    total[r] = total[r] * fade + jnp.sum(weight, -1, keepdims=True)
    acc[r] = acc[r] * fade[:, :1] + jnp.dot(
        weight.astype(jnp.bfloat16), value_rows, preferred_element_type=jnp.float32
    )


def absorb_blocks(blocks, first, valid, query_rows, keys, peak, total, acc, even, odd):
    def request_of(b):
        r = jnp.int32(0)
        for n in range(1, 4):
            r = r + jnp.where(b >= first[n], 1, 0)
        return r

    def scores_of(b):
        return lax.dot_general(
            query_rows[request_of(b)], keys[jnp.minimum(b, blocks - 1)], NT, preferred_element_type=jnp.float32
        )

    def take(b, scores):
        value_rows = keys[jnp.minimum(b, blocks - 1), :, :LAT]
        absorb(scores[...], key_limit(b * 8, valid), value_rows, peak, total, acc, request_of(b))

    even[...] = scores_of(0)

    def step(n, _):
        odd[...] = scores_of(2 * n + 1)
        take(2 * n, even)
        even[...] = scores_of(2 * n + 2)
        take(2 * n + 1, odd)
        return 0

    lax.fori_loop(0, (first[4] + 1) // 2, step, 0)


def resident_kernel(
    lists, lengths, queries, fresh, cache,
    query_rows, peak, total, acc, slot_row, rec_valid, rec_first,
    keys, even, odd, head_rows, res_page, res_valid, res_first,
):
    for i in range(RES_BLOCKS * 8):
        res_page[i] = 0
    for i in range(RES_SPARE):
        res_valid[i] = 0
    for i in range(REC_SPARE):
        rec_valid[i] = 0
    for i in range(17):
        slot_row[i] = 0
    res_at, rec_at = jnp.int32(0), jnp.int32(0)
    for r in range(4):
        res_first[r] = res_at // 8
        rec_first[r] = rec_at // 8
        length = lengths[r]

        def page(p, carry):
            res_at, rec_at = carry
            entry = lists[r, p]
            live = jnp.minimum(length - p * PAGE, PAGE)
            resident = entry < 64
            at = jnp.where(resident, res_at, RES_SPARE)
            res_page[at] = entry
            res_valid[at] = live
            at = jnp.where(resident, REC_SPARE, rec_at)
            rec_valid[at] = live
            slot_row[jnp.where(resident, 16, entry - 64)] = rec_at
            one = jnp.where(resident, 1, 0)
            return res_at + one, rec_at + 1 - one

        res_at, rec_at = lax.fori_loop(0, (length + PAGE - 1) // PAGE, page, (res_at, rec_at))
        res_at = (res_at + 7) // 8 * 8
        rec_at = (rec_at + 7) // 8 * 8
    res_first[4] = res_at // 8
    rec_first[4] = rec_at // 8

    to, of = iota((128, 128), 0), iota((128, 128), 1)
    wanted = ((to >> 1) & 15) * 8 + (to >> 5) * 2 + (to & 1)
    order = (wanted == of).astype(jnp.float32).astype(jnp.bfloat16)
    for g in range(HEADS // 16):
        for n in range(8):
            two = queries[:, (g * 8 + n) * PAIR : (g * 8 + n + 1) * PAIR].astype(jnp.float32)
            head_rows[pl.ds(n * 16, 16), :] = jnp.concatenate(
                [two[:, :KVW], two[:, KVW:]], 0
            ).astype(jnp.bfloat16)
        placed = jnp.dot(order, head_rows[...], preferred_element_type=jnp.float32).astype(jnp.bfloat16)
        for r in range(4):
            query_rows[r, g * 32 : g * 32 + 32, :] = placed[r * 32 : r * 32 + 32]

    new_keys = jnp.concatenate([fresh[...].astype(jnp.float32), jnp.zeros((120, KVW), jnp.float32)], 0).astype(jnp.bfloat16)
    for r in range(4):
        scores = lax.dot_general(query_rows[r], new_keys, NT, preferred_element_type=jnp.float32) * EXPONENT
        column, j = iota((ROWS, 128), 1), iota((ROWS, 128), 0) & 1
        seen = (column == 2 * r) | ((column == 2 * r + 1) & (j == 1))
        scores = jnp.where(seen, scores, LOW)
        top = jnp.max(scores, -1, keepdims=True)
        weight = jnp.exp2(scores - top)
        peak[r] = jnp.broadcast_to(top, (ROWS, 128))
        total[r] = jnp.broadcast_to(jnp.sum(weight, -1, keepdims=True), (ROWS, 128))
        acc[r] = jnp.dot(weight.astype(jnp.bfloat16), new_keys[:, :LAT], preferred_element_type=jnp.float32)

    pick = []
    sub, lane = iota((8, 64), 0), iota((8, 64), 1)
    for b in range(RES_BLOCKS):
        source = jnp.zeros((8, 64), jnp.int32)
        for i in range(8):
            source = jnp.where(sub == i, res_page[b * 8 + i], source)
        pick.append((source == lane).astype(jnp.float32))
    pick.append(jnp.zeros((8, 64), jnp.float32))
    pick = jnp.concatenate(pick, 0).astype(jnp.bfloat16)
    lay_keys(pick, lambda lanes: cache[:, lanes], keys, RES_BLOCKS)

    absorb_blocks(RES_BLOCKS, res_first, res_valid, query_rows, keys, peak, total, acc, even, odd)


def attend_resident(lists, lengths, queries, fresh, cache):
    smem, vmem = pl.BlockSpec(memory_space=pltpu.SMEM), pl.BlockSpec(memory_space=pltpu.VMEM)
    shapes = [
        jax.ShapeDtypeStruct((4, ROWS, KVW), jnp.bfloat16),
        jax.ShapeDtypeStruct((4, ROWS, 128), jnp.float32),
        jax.ShapeDtypeStruct((4, ROWS, 128), jnp.float32),
        jax.ShapeDtypeStruct((4, ROWS, LAT), jnp.float32),
        jax.ShapeDtypeStruct((24,), jnp.int32),
        jax.ShapeDtypeStruct((REC_SPARE + 8,), jnp.int32),
        jax.ShapeDtypeStruct((8,), jnp.int32),
    ]
    return pl.pallas_call(
        resident_kernel,
        out_shape=shapes,
        in_specs=[smem, smem, vmem, vmem, vmem],
        out_specs=[vmem] * 4 + [smem] * 3,
        scratch_shapes=[
            pltpu.VMEM((RES_BLOCKS, KEYS, KVW), jnp.bfloat16),
            pltpu.VMEM((ROWS, KEYS), jnp.float32),
            pltpu.VMEM((ROWS, KEYS), jnp.float32),
            pltpu.VMEM((128, KVW), jnp.bfloat16),
            pltpu.SMEM((RES_SPARE + 8,), jnp.int32),
            pltpu.SMEM((RES_SPARE + 8,), jnp.int32),
            pltpu.SMEM((8,), jnp.int32),
        ],
        compiler_params=pltpu.CompilerParams(vmem_limit_bytes=20 * MIB),
        cost_estimate=pl.CostEstimate(flops=8_000_000_000, bytes_accessed=12_000_000, transcendentals=2_000_000),
        name="attend_resident",
    )(lists, lengths, queries, fresh, cache)


def received_kernel(
    route, slot_row, rec_valid, rec_first,
    box1, box2, box3, own, query_rows, peak_in, total_in, acc_in,
    out, keys, even, odd, peak, total, acc, sems,
):
    state = [
        pltpu.make_async_copy(kept, held, sems.at[n])
        for n, (kept, held) in enumerate(((peak_in, peak), (total_in, total), (acc_in, acc)))
    ]
    for copy in state:
        copy.start()
    boxes = (box1, box2, box3)
    cols = iota((24, 128), 1)
    slots = jnp.concatenate([box[:, PAGE_WIDTH:].astype(jnp.float32) for box in boxes], 0)
    arrived = jnp.zeros((24, 128), jnp.float32)
    for n in range(16):
        arrived = jnp.where((slots == float(n)) & (cols == slot_row[n]), 1.0, arrived)
    rows, cols = iota((16, 128), 0), iota((16, 128), 1)
    kept = jnp.zeros((16, 128), jnp.float32)
    for i in range(16):
        target = jnp.where(route[i] >> 4 == 0, slot_row[route[i] & 15], -1)
        kept = jnp.where((rows == i) & (cols == target), 1.0, kept)
    place_of = jnp.concatenate([arrived, kept, jnp.zeros((88, 128), jnp.float32)], 0)
    pick = place_of.T[:48, :48].astype(jnp.bfloat16)

    def source(lanes):
        parts = [box[:, lanes].astype(jnp.float32) for box in boxes]
        parts.append(own[:, lanes].astype(jnp.float32))
        parts.append(jnp.zeros((8, PAIR), jnp.float32))
        return jnp.concatenate(parts, 0).astype(jnp.bfloat16)

    lay_keys(pick, source, keys, REC_BLOCKS)
    for copy in state:
        copy.wait()
    absorb_blocks(REC_BLOCKS, rec_first, rec_valid, query_rows, keys, peak, total, acc, even, odd)
    for t in range(0, 32, 8):
        parts = []
        for r in range(4):
            part = acc[r, t * 8 : t * 8 + 64] * (1.0 / total[r, t * 8 : t * 8 + 64, :1])
            parts.append(part.reshape(8, 8, LAT))
        out[t : t + 8] = jnp.concatenate(parts, 1).astype(jnp.bfloat16)


def attend_received(route, plan, boxes, own, state):
    smem, vmem = pl.BlockSpec(memory_space=pltpu.SMEM), pl.BlockSpec(memory_space=pltpu.VMEM)
    return pl.pallas_call(
        received_kernel,
        out_shape=jax.ShapeDtypeStruct((32, 32, LAT), jnp.bfloat16),
        in_specs=[smem] * 4 + [vmem] * 8,
        out_specs=vmem,
        scratch_shapes=[
            pltpu.VMEM((REC_BLOCKS, KEYS, KVW), jnp.bfloat16),
            pltpu.VMEM((ROWS, KEYS), jnp.float32),
            pltpu.VMEM((ROWS, KEYS), jnp.float32),
            pltpu.VMEM((4, ROWS, 128), jnp.float32),
            pltpu.VMEM((4, ROWS, 128), jnp.float32),
            pltpu.VMEM((4, ROWS, LAT), jnp.float32),
            pltpu.SemaphoreType.DMA((3,)),
        ],
        compiler_params=pltpu.CompilerParams(vmem_limit_bytes=20 * MIB),
        name="attend_received",
    )(route, *plan, *boxes, own, *state)


def product(rows, weights, store):
    start = 0
    for weight in weights:
        for at in range(0, weight.shape[1], PRODUCT_WIDTH):
            got = jnp.dot(rows, weight[:, at : at + PRODUCT_WIDTH], preferred_element_type=jnp.float32)
            store(slice(start + at, start + at + PRODUCT_WIDTH), got)
        start += weight.shape[1]


def store_blocks(outs):
    def store(lanes, got):
        for k, out in enumerate(outs):
            out[:, lanes] = got[k * 32 : k * 32 + 32].astype(out.dtype)

    return store


def stage_kernel(_after, weight, *refs):
    staged, sems = refs[:-1], refs[-1]
    copies, start = [], 0
    for n, out in enumerate(staged):
        width = out.shape[1]
        copies.append(pltpu.make_async_copy(weight.at[:, pl.ds(start, width)], out, sems.at[n]))
        copies[n].start()
        start += width
    for copy in copies:
        copy.wait()


def stage(after, weight):
    anywhere = pl.BlockSpec(memory_space=pl.ANY)
    return pl.pallas_call(
        stage_kernel,
        out_shape=[jax.ShapeDtypeStruct((weight.shape[0], width), weight.dtype) for width in CUTS],
        in_specs=[anywhere] * 2,
        out_specs=[pl.BlockSpec(memory_space=pltpu.VMEM)] * len(CUTS),
        scratch_shapes=[pltpu.SemaphoreType.DMA((len(CUTS),))],
        compiler_params=pltpu.CompilerParams(vmem_limit_bytes=4 * MIB),
        cost_estimate=pl.CostEstimate(flops=4_000_000_000, bytes_accessed=15_000_000, transcendentals=0),
        name="stage",
    )(after, weight)


def values_kernel(order, rows, value_up, mine, theirs):
    wide = jnp.concatenate([value_up[h] for h in range(4)], 1)
    all_heads = jnp.dot(rows[...], wide, preferred_element_type=jnp.float32)
    at, column = iota((1024, 512), 0), iota((1024, 512), 1)
    own_head = ((at >> 1) & 3) == (column >> 7)
    values = jnp.where(own_head, all_heads, 0.0).astype(jnp.bfloat16)
    n = iota((256, 1024), 1)
    token = (n >> 5) * 8 + ((n >> 3) & 3) * 2 + (n & 1)
    pick = (order[...] == token).astype(jnp.float32).astype(jnp.bfloat16)
    values = jnp.dot(pick, values, preferred_element_type=jnp.float32).astype(jnp.bfloat16)
    mine[...] = values[:128]
    theirs[...] = values[128:]


def find_values(order, rows, value_up):
    vmem = pl.BlockSpec(memory_space=pltpu.VMEM)
    return pl.pallas_call(
        values_kernel,
        out_shape=[jax.ShapeDtypeStruct((128, 512), jnp.bfloat16)] * 2,
        in_specs=[vmem] * 3,
        out_specs=[vmem] * 2,
        compiler_params=pltpu.CompilerParams(vmem_limit_bytes=16 * MIB),
        cost_estimate=pl.CostEstimate(flops=4_000_000_000, bytes_accessed=4_000_000, transcendentals=0),
        name="values",
    )(order, rows, value_up)


def project_kernel(rows, *refs):
    product(rows[...], refs[:-4], store_blocks(refs[-4:]))


def project(rows, weights, dtype):
    vmem = pl.BlockSpec(memory_space=pltpu.VMEM)
    width = sum(weight.shape[1] for weight in weights)
    return pl.pallas_call(
        project_kernel,
        out_shape=[jax.ShapeDtypeStruct((32, width), dtype)] * 4,
        in_specs=[vmem] * (1 + len(weights)),
        out_specs=[vmem] * 4,
        compiler_params=pltpu.CompilerParams(vmem_limit_bytes=16 * MIB),
        cost_estimate=pl.CostEstimate(flops=1_000_000_000, bytes_accessed=11_000_000, transcendentals=0),
        name="project",
    )(rows, *weights)


def hidden_kernel(*refs):
    rows, (gate_weight, up_weight, down_weight, act_out), theirs = refs[:8], refs[8:12], refs[12:16]
    gate, up_part = refs[16:]
    width = HIDDEN_WIDTH
    for n in range(rows[0].shape[1] // width):
        lanes = slice(n * width, n * width + width)
        block = jnp.concatenate([row[:, lanes] for row in rows], 0)
        for total, weight in ((gate, gate_weight), (up_part, up_weight)):
            got = lax.dot_general(weight[:, lanes], block, NT, preferred_element_type=jnp.float32)
            total[...] = got if n == 0 else total[...] + got
    g = gate[...]
    act = (g / (1.0 + jnp.exp(-g)) * up_part[...]).T.astype(jnp.bfloat16)
    act_out[...] = act[:128]
    product(act[128:], [down_weight], store_blocks(theirs))


def hidden_units(rows, gate_weight, up_weight, down_weight):
    vmem = pl.BlockSpec(memory_space=pltpu.VMEM)
    units, width = down_weight.shape
    return pl.pallas_call(
        hidden_kernel,
        out_shape=[jax.ShapeDtypeStruct((128, units), jnp.bfloat16)]
        + [jax.ShapeDtypeStruct((32, width), jnp.bfloat16)] * 4,
        in_specs=[vmem] * 11,
        out_specs=[vmem] * 5,
        scratch_shapes=[pltpu.VMEM((units, 256), jnp.float32)] * 2,
        compiler_params=pltpu.CompilerParams(vmem_limit_bytes=20 * MIB),
        cost_estimate=pl.CostEstimate(flops=3_000_000_000, bytes_accessed=18_000_000, transcendentals=80_000),
        name="hidden_units",
    )(*rows, gate_weight.T, up_weight.T, down_weight)


def shards(
    residual,
    queries,
    fresh_latents,
    cache_pages,
    prefill_pages,
    prefill_owner,
    prefill_slot,
    page_lists,
    context_len,
    value_up,
    out_proj,
    norm_gain,
    gate_weight,
    up_weight,
    down_weight,
):
    route = ((prefill_owner - lax.axis_index("grp")) & 3) * 16 + prefill_slot
    boxes = outbox(route, prefill_pages)
    boxes = {k: lax.ppermute(boxes[k - 1], "grp", [(g, (g + k) % 4) for g in range(4)]) for k in (1, 3, 2)}
    boxes = [boxes[k] for k in (1, 2, 3)]
    *state, slot_row, rec_valid, rec_first = attend_resident(
        page_lists, context_len, queries, fresh_latents, cache_pages
    )
    attended = attend_received(
        route, (slot_row, rec_valid, rec_first), boxes, prefill_pages, state
    )
    out_proj = stage(attended, out_proj)
    by_heads = lax.all_to_all(attended, "tp", split_axis=0, concat_axis=0, tiled=True)
    mine, theirs = find_values(token_order()[:, None], by_heads.reshape(1024, LAT), value_up)
    theirs = project(theirs, out_proj, jnp.bfloat16)
    terms = reduce_first(project(mine, out_proj, jnp.float32), theirs)
    hidden, normed = settle(terms, residual, norm_gain)
    act, *theirs = hidden_units(gather_first(normed), gate_weight, up_weight, down_weight)
    mlp = reduce_second(reduce_first(project(act, [down_weight], jnp.float32), theirs))
    return (hidden.astype(jnp.float32) + mlp).astype(jnp.bfloat16)


def solution(mesh):
    placed = (
        P(("grp", "tp"), None),
        P(("grp", "tp"), None),
        P(("grp", "tp"), None),
        P(("grp", "tp"), None),
        P(("grp", "tp"), None),
        P(("grp", "tp")),
        P(("grp", "tp")),
        P(("grp", "tp"), None),
        P(("grp", "tp")),
        P("tp", None, None),
        P("tp", None),
        P(),
        P(None, "tp"),
        P(None, "tp"),
        P("tp", None),
    )
    return jax.shard_map(
        shards, mesh=mesh, in_specs=placed, out_specs=P(("grp", "tp"), None), check_vma=False
    )
```

```python
import math

import jax
import jax.numpy as jnp
from jax import lax
from jax.experimental import pallas as pl
from jax.experimental.pallas import tpu as pltpu
from jax.sharding import PartitionSpec as P

HEADS = 128
LAT = 512
ROPE = 64
HEADV = 128
PAGE = 64
KVW = 576
MOST = 8
PAGE_WIDTH = PAGE * KVW
PAIR = 2 * KVW
RES_BLOCKS = 11
UNROLL = 16
CUTS = (1792, 5376)
PRODUCT_WIDTH = 256
HIDDEN_WIDTH = 1792
REC_BLOCKS = 5
RES_SPARE = (RES_BLOCKS + 1) * 8
REC_SPARE = (REC_BLOCKS + 1) * 8
KEYS = 8 * PAGE
LOW = -1e30
EXPONENT = (HEADV + ROPE) ** (-0.5) * math.log2(math.e)
ROWS = 2 * HEADS
NT = (((1,), (1,)), ((), ()))
MIB = 1024 * 1024


def chip_pairs(step0, step1):
    pairs = []
    for y in range(4):
        for x in range(4):
            for core, (dy, dx, flip) in enumerate((step0, step1)):
                there = (((y + dy) % 4) * 4 + (x + dx) % 4) * 2 + (core ^ flip)
                pairs.append(((y * 4 + x) * 2 + core, there))
    return pairs


def swap_cores(block):
    return lax.ppermute(block, "tp", chip_pairs((0, 0, 1), (0, 0, 1)))


def along_first(block, k):
    return lax.ppermute(block, "tp", chip_pairs((0, k, 0), (k, 0, 0)))


def along_second(block, k):
    return lax.ppermute(block, "tp", chip_pairs((k, 0, 0), (0, k, 0)))


def token_order():
    t = lax.axis_index("tp")
    y, x, core = t // 8, (t // 2) % 4, t % 2
    row = jnp.arange(256, dtype=jnp.int32)
    owner_core = jnp.where(row // 128 == 0, core, 1 - core)
    k1, k2, i = (row // 32) % 4, (row // 8) % 4, row % 8
    dy = jnp.where(owner_core == 0, k2, k1)
    dx = jnp.where(owner_core == 0, k1, k2)
    return ((((y + dy) % 4) * 4 + (x + dx) % 4) * 2 + owner_core) * 8 + i


def add_up(own, others):
    total = own.astype(jnp.float32)
    for other in others:
        total = total + other.astype(jnp.float32)
    return total


def reduce_first(mine, theirs):
    got = {k: swap_cores(theirs[k]) for k in (2, 1, 3, 0)}
    chunks = {k: add_up(mine[k], [got[k]]).astype(jnp.bfloat16) for k in (2, 1, 3)}
    return [mine[0], got[0]] + [along_first(chunks[k], k) for k in (2, 1, 3)]


def reduce_second(terms):
    chunks = add_up(terms[0], terms[1:]).reshape(4, 8, -1)
    arrived = [along_second(chunks[k].astype(jnp.bfloat16), k) for k in (2, 1, 3)]
    return add_up(chunks[0], arrived)


def share_kernel(residual, *refs):
    terms, (total, sent) = refs[:-2], refs[-2:]
    for n in range(0, total.shape[1], 1024):
        lanes = slice(n, n + 1024)
        own = terms[0][:, lanes]
        for term in terms[1:]:
            own = own + term[:, lanes].astype(jnp.float32)
        first = own[:8] + residual[:, lanes].astype(jnp.float32)
        own = jnp.concatenate([first, own[8:]], 0)
        total[:, lanes] = own
        sent[:, lanes] = own.astype(jnp.bfloat16)


def settle_kernel(total, got1, got2, got3, norm_gain, hidden_out, normed, hidden):
    width = total.shape[1]
    squares = jnp.zeros((32, 1), jnp.float32)
    for n in range(0, width, 1024):
        lanes = slice(n, n + 1024)
        block = total[:, lanes]
        for k, got in ((1, got1), (2, got2), (3, got3)):
            got = got[:, lanes].astype(jnp.float32)
            block = block + jnp.concatenate([got[k * 8 :], got[: k * 8]], 0)
        block = block.astype(jnp.bfloat16)
        hidden_out[:, lanes] = block[:8]
        block = block.astype(jnp.float32)
        hidden[:, lanes] = block
        squares = squares + jnp.sum(block * block, -1, keepdims=True)
    spread = lax.rsqrt(squares * (1.0 / width) + 1e-06)
    for n in range(0, width, 1024):
        lanes = slice(n, n + 1024)
        gain = norm_gain[:, lanes].astype(jnp.float32)
        normed[:, lanes] = (hidden[:, lanes] * spread * gain).astype(jnp.bfloat16)


def settle(terms, residual, norm_gain):
    vmem = pl.BlockSpec(memory_space=pltpu.VMEM)
    params = pltpu.CompilerParams(vmem_limit_bytes=12 * MIB)
    shape = terms[0].shape
    total, sent = pl.pallas_call(
        share_kernel,
        out_shape=[jax.ShapeDtypeStruct(shape, jnp.float32), jax.ShapeDtypeStruct(shape, jnp.bfloat16)],
        in_specs=[vmem] * 6,
        out_specs=[vmem] * 2,
        compiler_params=params,
        name="share",
    )(residual, *terms)
    got = {k: along_second(sent, k) for k in (2, 1, 3)}
    return pl.pallas_call(
        settle_kernel,
        out_shape=[
            jax.ShapeDtypeStruct(residual.shape, jnp.bfloat16),
            jax.ShapeDtypeStruct(shape, jnp.bfloat16),
        ],
        in_specs=[vmem] * 5,
        out_specs=[vmem] * 2,
        scratch_shapes=[pltpu.VMEM(shape, jnp.float32)],
        compiler_params=params,
        name="settle",
    )(total, got[1], got[2], got[3], norm_gain[None, :])


def gather_first(rows):
    arrived = {k: along_first(rows, 4 - k) for k in (2, 1, 3)}
    mine = [rows] + [arrived[k] for k in (1, 2, 3)]
    return mine + [swap_cores(part) for part in mine]


def iota(shape, dim):
    return lax.broadcasted_iota(jnp.int32, shape, dim)


def outbox_kernel(route, pages, out1, out2, out3):
    outs = (out1, out2, out3)
    rows, cols = iota((32, 128), 0), iota((32, 128), 1)
    pick = jnp.zeros((32, 128), jnp.float32)
    slots = jnp.full((32, 128), 64, jnp.int32)
    counts = [jnp.int32(0)] * 4
    for i in range(16):
        step = route[i] >> 4
        rank = jnp.int32(0)
        for k in range(1, 4):
            rank = jnp.where(step == k, counts[k], rank)
            counts[k] = counts[k] + jnp.where(step == k, 1, 0)
        target = jnp.where(step == 0, -1, (step - 1) * MOST + rank)
        pick = jnp.where((rows == target) & (cols == i), 1.0, pick)
        slots = jnp.where(rows == target, route[i] & 15, slots)
    pick = pick[:, :16].astype(jnp.bfloat16)
    slots = slots.astype(jnp.float32).astype(jnp.bfloat16)

    def chunk(n, _):
        for u in range(UNROLL):
            lanes = pl.ds(pl.multiple_of((n * UNROLL + u) * PAIR, 128), PAIR)
            got = jnp.dot(pick, pages[:, lanes], preferred_element_type=jnp.float32)
            for k in range(3):
                outs[k][:, lanes] = got[k * 8 : k * 8 + 8].astype(jnp.bfloat16)
        return 0

    lax.fori_loop(0, PAGE // 2 // UNROLL, chunk, 0)
    for k in range(3):
        outs[k][:, PAGE_WIDTH:] = slots[k * 8 : k * 8 + 8]


def outbox(route, pages):
    smem, vmem = pl.BlockSpec(memory_space=pltpu.SMEM), pl.BlockSpec(memory_space=pltpu.VMEM)
    return pl.pallas_call(
        outbox_kernel,
        out_shape=[jax.ShapeDtypeStruct((MOST, PAGE_WIDTH + 128), jnp.bfloat16)] * 3,
        in_specs=[smem, vmem],
        out_specs=[vmem] * 3,
        compiler_params=pltpu.CompilerParams(vmem_limit_bytes=16 * MIB),
        name="outbox",
    )(route, pages)


def lay_keys(pick, source, keys, blocks):
    def chunk(n, _):
        for u in range(UNROLL):
            at = n * UNROLL + u
            lanes = pl.ds(pl.multiple_of(at * PAIR, 128), PAIR)
            got = jnp.dot(pick, source(lanes), preferred_element_type=jnp.float32)
            even = got[: blocks * 8, :KVW].reshape(blocks, 8, KVW)
            odd = got[: blocks * 8, KVW:].reshape(blocks, 8, KVW)
            both = jnp.concatenate([even, odd], 1).astype(jnp.bfloat16)
            keys[:, pl.ds(pl.multiple_of(at * 16, 16), 16), :] = both
        return 0

    lax.fori_loop(0, PAGE // 2 // UNROLL, chunk, 0)


def key_limit(first, valid):
    at = iota((8, KEYS), 1)
    limit = jnp.zeros((8, KEYS), jnp.int32)
    for i in range(8):
        limit = jnp.where((at & 7) == i, valid[first + i], limit)
    return ((at >> 3) < limit)[:1]


def absorb(scores, live, value_rows, peak, total, acc, r):
    scores = jnp.where(live, scores * EXPONENT, LOW)
    before = peak[r]
    top = jnp.maximum(before, jnp.max(scores, -1, keepdims=True))
    weight = jnp.exp2(scores - top[:, :1])
    fade = jnp.exp2(before - top)
    peak[r] = top
    total[r] = total[r] * fade + jnp.sum(weight, -1, keepdims=True)
    acc[r] = acc[r] * fade[:, :1] + jnp.dot(
        weight.astype(jnp.bfloat16), value_rows, preferred_element_type=jnp.float32
    )


def absorb_blocks(blocks, first, valid, query_rows, keys, peak, total, acc, even, odd):
    def request_of(b):
        r = jnp.int32(0)
        for n in range(1, 4):
            r = r + jnp.where(b >= first[n], 1, 0)
        return r

    def scores_of(b):
        return lax.dot_general(
            query_rows[request_of(b)], keys[jnp.minimum(b, blocks - 1)], NT, preferred_element_type=jnp.float32
        )

    def take(b, scores):
        value_rows = keys[jnp.minimum(b, blocks - 1), :, :LAT]
        absorb(scores[...], key_limit(b * 8, valid), value_rows, peak, total, acc, request_of(b))

    even[...] = scores_of(0)

    def step(n, _):
        odd[...] = scores_of(2 * n + 1)
        take(2 * n, even)
        even[...] = scores_of(2 * n + 2)
        take(2 * n + 1, odd)
        return 0

    lax.fori_loop(0, (first[4] + 1) // 2, step, 0)


def resident_kernel(
    lists, lengths, queries, fresh, cache,
    query_rows, peak, total, acc, slot_row, rec_valid, rec_first,
    keys, even, odd, head_rows, res_page, res_valid, res_first,
):
    for i in range(RES_BLOCKS * 8):
        res_page[i] = 0
    for i in range(RES_SPARE):
        res_valid[i] = 0
    for i in range(REC_SPARE):
        rec_valid[i] = 0
    for i in range(17):
        slot_row[i] = 0
    res_at, rec_at = jnp.int32(0), jnp.int32(0)
    for r in range(4):
        res_first[r] = res_at // 8
        rec_first[r] = rec_at // 8
        length = lengths[r]

        def page(p, carry):
            res_at, rec_at = carry
            entry = lists[r, p]
            live = jnp.minimum(length - p * PAGE, PAGE)
            resident = entry < 64
            at = jnp.where(resident, res_at, RES_SPARE)
            res_page[at] = entry
            res_valid[at] = live
            at = jnp.where(resident, REC_SPARE, rec_at)
            rec_valid[at] = live
            slot_row[jnp.where(resident, 16, entry - 64)] = rec_at
            one = jnp.where(resident, 1, 0)
            return res_at + one, rec_at + 1 - one

        res_at, rec_at = lax.fori_loop(0, (length + PAGE - 1) // PAGE, page, (res_at, rec_at))
        res_at = (res_at + 7) // 8 * 8
        rec_at = (rec_at + 7) // 8 * 8
    res_first[4] = res_at // 8
    rec_first[4] = rec_at // 8

    to, of = iota((128, 128), 0), iota((128, 128), 1)
    wanted = ((to >> 1) & 15) * 8 + (to >> 5) * 2 + (to & 1)
    order = (wanted == of).astype(jnp.float32).astype(jnp.bfloat16)
    for g in range(HEADS // 16):
        for n in range(8):
            two = queries[:, (g * 8 + n) * PAIR : (g * 8 + n + 1) * PAIR].astype(jnp.float32)
            head_rows[pl.ds(n * 16, 16), :] = jnp.concatenate(
                [two[:, :KVW], two[:, KVW:]], 0
            ).astype(jnp.bfloat16)
        placed = jnp.dot(order, head_rows[...], preferred_element_type=jnp.float32).astype(jnp.bfloat16)
        for r in range(4):
            query_rows[r, g * 32 : g * 32 + 32, :] = placed[r * 32 : r * 32 + 32]

    new_keys = jnp.concatenate([fresh[...].astype(jnp.float32), jnp.zeros((120, KVW), jnp.float32)], 0).astype(jnp.bfloat16)
    for r in range(4):
        scores = lax.dot_general(query_rows[r], new_keys, NT, preferred_element_type=jnp.float32) * EXPONENT
        column, j = iota((ROWS, 128), 1), iota((ROWS, 128), 0) & 1
        seen = (column == 2 * r) | ((column == 2 * r + 1) & (j == 1))
        scores = jnp.where(seen, scores, LOW)
        top = jnp.max(scores, -1, keepdims=True)
        weight = jnp.exp2(scores - top)
        peak[r] = jnp.broadcast_to(top, (ROWS, 128))
        total[r] = jnp.broadcast_to(jnp.sum(weight, -1, keepdims=True), (ROWS, 128))
        acc[r] = jnp.dot(weight.astype(jnp.bfloat16), new_keys[:, :LAT], preferred_element_type=jnp.float32)

    pick = []
    sub, lane = iota((8, 64), 0), iota((8, 64), 1)
    for b in range(RES_BLOCKS):
        source = jnp.zeros((8, 64), jnp.int32)
        for i in range(8):
            source = jnp.where(sub == i, res_page[b * 8 + i], source)
        pick.append((source == lane).astype(jnp.float32))
    pick.append(jnp.zeros((8, 64), jnp.float32))
    pick = jnp.concatenate(pick, 0).astype(jnp.bfloat16)
    lay_keys(pick, lambda lanes: cache[:, lanes], keys, RES_BLOCKS)

    absorb_blocks(RES_BLOCKS, res_first, res_valid, query_rows, keys, peak, total, acc, even, odd)


def attend_resident(lists, lengths, queries, fresh, cache):
    smem, vmem = pl.BlockSpec(memory_space=pltpu.SMEM), pl.BlockSpec(memory_space=pltpu.VMEM)
    shapes = [
        jax.ShapeDtypeStruct((4, ROWS, KVW), jnp.bfloat16),
        jax.ShapeDtypeStruct((4, ROWS, 128), jnp.float32),
        jax.ShapeDtypeStruct((4, ROWS, 128), jnp.float32),
        jax.ShapeDtypeStruct((4, ROWS, LAT), jnp.float32),
        jax.ShapeDtypeStruct((24,), jnp.int32),
        jax.ShapeDtypeStruct((REC_SPARE + 8,), jnp.int32),
        jax.ShapeDtypeStruct((8,), jnp.int32),
    ]
    return pl.pallas_call(
        resident_kernel,
        out_shape=shapes,
        in_specs=[smem, smem, vmem, vmem, vmem],
        out_specs=[vmem] * 4 + [smem] * 3,
        scratch_shapes=[
            pltpu.VMEM((RES_BLOCKS, KEYS, KVW), jnp.bfloat16),
            pltpu.VMEM((ROWS, KEYS), jnp.float32),
            pltpu.VMEM((ROWS, KEYS), jnp.float32),
            pltpu.VMEM((128, KVW), jnp.bfloat16),
            pltpu.SMEM((RES_SPARE + 8,), jnp.int32),
            pltpu.SMEM((RES_SPARE + 8,), jnp.int32),
            pltpu.SMEM((8,), jnp.int32),
        ],
        compiler_params=pltpu.CompilerParams(vmem_limit_bytes=20 * MIB),
        cost_estimate=pl.CostEstimate(flops=8_000_000_000, bytes_accessed=12_000_000, transcendentals=2_000_000),
        name="attend_resident",
    )(lists, lengths, queries, fresh, cache)


def received_kernel(
    route, slot_row, rec_valid, rec_first,
    box1, box2, box3, own, query_rows, peak_in, total_in, acc_in,
    out, keys, even, odd, peak, total, acc, sems,
):
    state = [
        pltpu.make_async_copy(kept, held, sems.at[n])
        for n, (kept, held) in enumerate(((peak_in, peak), (total_in, total), (acc_in, acc)))
    ]
    for copy in state:
        copy.start()
    boxes = (box1, box2, box3)
    cols = iota((24, 128), 1)
    slots = jnp.concatenate([box[:, PAGE_WIDTH:].astype(jnp.float32) for box in boxes], 0)
    arrived = jnp.zeros((24, 128), jnp.float32)
    for n in range(16):
        arrived = jnp.where((slots == float(n)) & (cols == slot_row[n]), 1.0, arrived)
    rows, cols = iota((16, 128), 0), iota((16, 128), 1)
    kept = jnp.zeros((16, 128), jnp.float32)
    for i in range(16):
        target = jnp.where(route[i] >> 4 == 0, slot_row[route[i] & 15], -1)
        kept = jnp.where((rows == i) & (cols == target), 1.0, kept)
    place_of = jnp.concatenate([arrived, kept, jnp.zeros((88, 128), jnp.float32)], 0)
    pick = place_of.T[:48, :48].astype(jnp.bfloat16)

    def source(lanes):
        parts = [box[:, lanes].astype(jnp.float32) for box in boxes]
        parts.append(own[:, lanes].astype(jnp.float32))
        parts.append(jnp.zeros((8, PAIR), jnp.float32))
        return jnp.concatenate(parts, 0).astype(jnp.bfloat16)

    lay_keys(pick, source, keys, REC_BLOCKS)
    for copy in state:
        copy.wait()
    absorb_blocks(REC_BLOCKS, rec_first, rec_valid, query_rows, keys, peak, total, acc, even, odd)
    for t in range(0, 32, 8):
        parts = []
        for r in range(4):
            part = acc[r, t * 8 : t * 8 + 64] * (1.0 / total[r, t * 8 : t * 8 + 64, :1])
            parts.append(part.reshape(8, 8, LAT))
        out[t : t + 8] = jnp.concatenate(parts, 1).astype(jnp.bfloat16)


def attend_received(route, plan, boxes, own, state):
    smem, vmem = pl.BlockSpec(memory_space=pltpu.SMEM), pl.BlockSpec(memory_space=pltpu.VMEM)
    return pl.pallas_call(
        received_kernel,
        out_shape=jax.ShapeDtypeStruct((32, 32, LAT), jnp.bfloat16),
        in_specs=[smem] * 4 + [vmem] * 8,
        out_specs=vmem,
        scratch_shapes=[
            pltpu.VMEM((REC_BLOCKS, KEYS, KVW), jnp.bfloat16),
            pltpu.VMEM((ROWS, KEYS), jnp.float32),
            pltpu.VMEM((ROWS, KEYS), jnp.float32),
            pltpu.VMEM((4, ROWS, 128), jnp.float32),
            pltpu.VMEM((4, ROWS, 128), jnp.float32),
            pltpu.VMEM((4, ROWS, LAT), jnp.float32),
            pltpu.SemaphoreType.DMA((3,)),
        ],
        compiler_params=pltpu.CompilerParams(vmem_limit_bytes=20 * MIB),
        name="attend_received",
    )(route, *plan, *boxes, own, *state)


def product(rows, weights, store):
    start = 0
    for weight in weights:
        for at in range(0, weight.shape[1], PRODUCT_WIDTH):
            got = jnp.dot(rows, weight[:, at : at + PRODUCT_WIDTH], preferred_element_type=jnp.float32)
            store(slice(start + at, start + at + PRODUCT_WIDTH), got)
        start += weight.shape[1]


def store_blocks(outs):
    def store(lanes, got):
        for k, out in enumerate(outs):
            out[:, lanes] = got[k * 32 : k * 32 + 32].astype(out.dtype)

    return store


def stage_kernel(_after, weight, *refs):
    staged, sems = refs[:-1], refs[-1]
    copies, start = [], 0
    for n, out in enumerate(staged):
        width = out.shape[1]
        copies.append(pltpu.make_async_copy(weight.at[:, pl.ds(start, width)], out, sems.at[n]))
        copies[n].start()
        start += width
    for copy in copies:
        copy.wait()


def stage(after, weight):
    anywhere = pl.BlockSpec(memory_space=pl.ANY)
    return pl.pallas_call(
        stage_kernel,
        out_shape=[jax.ShapeDtypeStruct((weight.shape[0], width), weight.dtype) for width in CUTS],
        in_specs=[anywhere] * 2,
        out_specs=[pl.BlockSpec(memory_space=pltpu.VMEM)] * len(CUTS),
        scratch_shapes=[pltpu.SemaphoreType.DMA((len(CUTS),))],
        compiler_params=pltpu.CompilerParams(vmem_limit_bytes=4 * MIB),
        cost_estimate=pl.CostEstimate(flops=4_000_000_000, bytes_accessed=15_000_000, transcendentals=0),
        name="stage",
    )(after, weight)


def values_kernel(order, rows, value_up, mine, theirs):
    wide = jnp.concatenate([value_up[h] for h in range(4)], 1)
    all_heads = jnp.dot(rows[...], wide, preferred_element_type=jnp.float32)
    at, column = iota((1024, 512), 0), iota((1024, 512), 1)
    own_head = ((at >> 1) & 3) == (column >> 7)
    values = jnp.where(own_head, all_heads, 0.0).astype(jnp.bfloat16)
    n = iota((256, 1024), 1)
    token = (n >> 5) * 8 + ((n >> 3) & 3) * 2 + (n & 1)
    pick = (order[...] == token).astype(jnp.float32).astype(jnp.bfloat16)
    values = jnp.dot(pick, values, preferred_element_type=jnp.float32).astype(jnp.bfloat16)
    mine[...] = values[:128]
    theirs[...] = values[128:]


def find_values(order, rows, value_up):
    vmem = pl.BlockSpec(memory_space=pltpu.VMEM)
    return pl.pallas_call(
        values_kernel,
        out_shape=[jax.ShapeDtypeStruct((128, 512), jnp.bfloat16)] * 2,
        in_specs=[vmem] * 3,
        out_specs=[vmem] * 2,
        compiler_params=pltpu.CompilerParams(vmem_limit_bytes=16 * MIB),
        cost_estimate=pl.CostEstimate(flops=4_000_000_000, bytes_accessed=4_000_000, transcendentals=0),
        name="values",
    )(order, rows, value_up)


def project_kernel(rows, *refs):
    product(rows[...], refs[:-4], store_blocks(refs[-4:]))


def project(rows, weights, dtype):
    vmem = pl.BlockSpec(memory_space=pltpu.VMEM)
    width = sum(weight.shape[1] for weight in weights)
    return pl.pallas_call(
        project_kernel,
        out_shape=[jax.ShapeDtypeStruct((32, width), dtype)] * 4,
        in_specs=[vmem] * (1 + len(weights)),
        out_specs=[vmem] * 4,
        compiler_params=pltpu.CompilerParams(vmem_limit_bytes=16 * MIB),
        cost_estimate=pl.CostEstimate(flops=1_000_000_000, bytes_accessed=11_000_000, transcendentals=0),
        name="project",
    )(rows, *weights)


def hidden_kernel(*refs):
    rows, (gate_weight, up_weight, down_weight, act_out), theirs = refs[:8], refs[8:12], refs[12:16]
    gate, up_part = refs[16:]
    width = HIDDEN_WIDTH
    for n in range(rows[0].shape[1] // width):
        lanes = slice(n * width, n * width + width)
        block = jnp.concatenate([row[:, lanes] for row in rows], 0)
        for total, weight in ((gate, gate_weight), (up_part, up_weight)):
            got = lax.dot_general(weight[:, lanes], block, NT, preferred_element_type=jnp.float32)
            total[...] = got if n == 0 else total[...] + got
    g = gate[...]
    act = (g / (1.0 + jnp.exp(-g)) * up_part[...]).T.astype(jnp.bfloat16)
    act_out[...] = act[:128]
    product(act[128:], [down_weight], store_blocks(theirs))


def hidden_units(rows, gate_weight, up_weight, down_weight):
    vmem = pl.BlockSpec(memory_space=pltpu.VMEM)
    units, width = down_weight.shape
    return pl.pallas_call(
        hidden_kernel,
        out_shape=[jax.ShapeDtypeStruct((128, units), jnp.bfloat16)]
        + [jax.ShapeDtypeStruct((32, width), jnp.bfloat16)] * 4,
        in_specs=[vmem] * 11,
        out_specs=[vmem] * 5,
        scratch_shapes=[pltpu.VMEM((units, 256), jnp.float32)] * 2,
        compiler_params=pltpu.CompilerParams(vmem_limit_bytes=20 * MIB),
        cost_estimate=pl.CostEstimate(flops=3_000_000_000, bytes_accessed=18_000_000, transcendentals=80_000),
        name="hidden_units",
    )(*rows, gate_weight.T, up_weight.T, down_weight)


def shards(
    residual,
    queries,
    fresh_latents,
    cache_pages,
    prefill_pages,
    prefill_owner,
    prefill_slot,
    page_lists,
    context_len,
    value_up,
    out_proj,
    norm_gain,
    gate_weight,
    up_weight,
    down_weight,
):
    route = ((prefill_owner - lax.axis_index("grp")) & 3) * 16 + prefill_slot
    boxes = outbox(route, prefill_pages)
    boxes = {k: lax.ppermute(boxes[k - 1], "grp", [(g, (g + k) % 4) for g in range(4)]) for k in (1, 3, 2)}
    boxes = [boxes[k] for k in (1, 2, 3)]
    *state, slot_row, rec_valid, rec_first = attend_resident(
        page_lists, context_len, queries, fresh_latents, cache_pages
    )
    attended = attend_received(
        route, (slot_row, rec_valid, rec_first), boxes, prefill_pages, state
    )
    out_proj = stage(attended, out_proj)
    by_heads = lax.all_to_all(attended, "tp", split_axis=0, concat_axis=0, tiled=True)
    mine, theirs = find_values(token_order()[:, None], by_heads.reshape(1024, LAT), value_up)
    theirs = project(theirs, out_proj, jnp.bfloat16)
    terms = reduce_first(project(mine, out_proj, jnp.float32), theirs)
    hidden, normed = settle(terms, residual, norm_gain)
    act, *theirs = hidden_units(gather_first(normed), gate_weight, up_weight, down_weight)
    mlp = reduce_second(reduce_first(project(act, [down_weight], jnp.float32), theirs))
    return (hidden.astype(jnp.float32) + mlp).astype(jnp.bfloat16)


def solution(mesh):
    placed = (
        P(("grp", "tp"), None),
        P(("grp", "tp"), None),
        P(("grp", "tp"), None),
        P(("grp", "tp"), None),
        P(("grp", "tp"), None),
        P(("grp", "tp")),
        P(("grp", "tp")),
        P(("grp", "tp"), None),
        P(("grp", "tp")),
        P("tp", None, None),
        P("tp", None),
        P(),
        P(None, "tp"),
        P(None, "tp"),
        P("tp", None),
    )
    return jax.shard_map(
        shards, mesh=mesh, in_specs=placed, out_specs=P(("grp", "tp"), None), check_vma=False
    )
```
